512 devices in a mesh: fsdp: 32 (over x, y), tensor: 16 (over z, core).
Axes of the slice: x: 4, y: 8, z: 8, core: 2. Of those that a mesh axis runs over, the one named last changes fastest.
Arguments:
- momentum: bfloat16 [8192, 26624], P('fsdp', 'tensor'), may hold values from -360 to 360
- weights: float32 [8192, 26624], P('fsdp', 'tensor'), may hold values from -3 to 3
- basis: float32 [26624, 128], P('tensor', 'fsdp'), may hold values from -6 to 6
Outputs:
- new_weights: float32 [8192, 26624], P('fsdp', 'tensor')
- new_momentum: bfloat16 [8192, 26624], P('fsdp', 'tensor')
- new_basis: float32 [26624, 128], P('tensor', 'fsdp')
The draws below stay inside these ranges and needn't reach their ends.
All inputs are finite; a program needn't handle non-finite values.
Results may differ from the reference program's by a relative error of at most 0.013.
Values may be sent and summed in bfloat16 or wider, within the bound.
A program may use at most 64 MiB of HBM per device.

```python
import math
import jax
import jax.numpy as jnp
from jax import lax

DW = 8192
FW = 26624
RANK = 128


def draw_momentum(key, part):
    key = jax.random.fold_in(key, 11)
    first, second, third, fourth, fifth = jax.random.split(key, 5)
    inner = 2 * RANK
    left_factor = jax.random.truncated_normal(first, -4.0, 4.0, (DW, inner), jnp.float32)
    right_factor = jax.random.truncated_normal(second, -4.0, 4.0, (FW, inner), jnp.float32)
    lowest = 0.03
    noise = 0.05 * jax.random.truncated_normal(fifth, -4.0, 4.0, (DW, FW), jnp.float32)
    spread = math.log(10.0)
    edge = 4.0
    decay = lowest ** (jnp.arange(inner, dtype=jnp.float32) / (inner - 1))
    decay = decay / jnp.sqrt(jnp.sum(decay * decay))
    structured = jnp.dot(left_factor * decay[None, :], right_factor.T, precision=lax.Precision.HIGHEST)
    values = jnp.clip(structured + noise, -edge, edge)
    column_scale = jnp.exp(jax.random.uniform(third, (1, FW), jnp.float32, 0.0, spread))
    rising = 1.0 + 2.0 * jnp.arange(FW, dtype=jnp.float32)[None, :] / FW
    row_scale = jnp.exp(jax.random.uniform(fourth, (DW, 1), jnp.float32, 0.0, math.log(3.0)))
    return (values * column_scale * rising * row_scale).astype(jnp.bfloat16)


def block_scale(own_key, dims, cuts, low, largest):
    loudness, own = 1.0, jax.random.fold_in(own_key, 6)
    for dim, parts in cuts:
        heights = jnp.exp(jax.random.uniform(jax.random.fold_in(own, dim), (parts,), jnp.float32, low / len(cuts), largest / len(cuts)))
        loudness = loudness * jnp.repeat(heights, dims[dim] // parts).reshape([-1 if axis == dim else 1 for axis in range(len(dims))])
    return loudness


def gaussian(key, shape, scale, reach, pieces=(), kind=jnp.bfloat16):
    result = scale * jax.random.normal(key, shape, jnp.float32)
    if pieces:
        result = result * block_scale(key, shape, pieces, -0.22, 0.18)
    return jnp.clip(result, -reach, reach).astype(kind)


def setup_inputs(seed: int = 0) -> dict:
    splits = jax.random.split(jax.random.key(seed), 4)
    return {
        "momentum": draw_momentum(jax.random.fold_in(splits[3], 71), 0),
        "weights": gaussian(splits[1], (DW, FW), 0.2, 3.0, ((0, 32), (1, 16)), jnp.float32),
        "basis": gaussian(splits[2], (FW, RANK), 1.0, 6.0, ((0, 16), (1, 32)), jnp.float32),
    }


HIGH = lax.Precision.HIGHEST

def reference(momentum, weights, basis):
    basis_half = basis.astype(jnp.bfloat16)
    projected = jnp.dot(momentum.astype(jnp.float32), basis_half.astype(jnp.float32), preferred_element_type=jnp.float32)
    gram_matrix = jnp.dot(projected.T, projected, precision=HIGH)
    factor = jnp.linalg.cholesky(gram_matrix)
    ortho = lax.linalg.triangular_solve(factor, projected, left_side=False, lower=True, transpose_a=True)
    ortho_half = ortho.astype(jnp.bfloat16)
    transposed = lax.dot_general(momentum.astype(jnp.float32), ortho_half.astype(jnp.float32), (((0,), (0,)), ((), ())), preferred_element_type=jnp.float32)
    squares = lax.optimization_barrier(jnp.sum(transposed * transposed, axis=0))
    new_basis = transposed * lax.rsqrt(squares / FW + 1e-06)
    feedback = lax.dot_general(ortho, transposed, (((1,), (1,)), ((), ())), precision=HIGH)
    new_momentum = (momentum.astype(jnp.float32) - 0.05 * feedback).astype(jnp.bfloat16)
    update = lax.dot_general(ortho, new_basis, (((1,), (1,)), ((), ())), precision=HIGH)
    new_weights = weights - 0.02 * math.sqrt(DW / RANK) * update
    return (new_weights, new_momentum, new_basis)
```

```python
import functools
import math

import jax
import jax.numpy as jnp
from jax import lax
from jax.experimental import pallas as pl
from jax.experimental.pallas import tpu as pltpu
from jax.sharding import PartitionSpec as P

DW = 8192
FW = 26624
RANK = 128
ROWS = 256
COLS = 1664
NX, NY, NZ = 4, 8, 8
QUARTER = COLS // NX
SLOT = 64

HIGH = lax.Precision.HIGHEST
MESH = pl.DeviceIdType.MESH
F32 = jnp.float32
BF16 = jnp.bfloat16


def spread_row(a, k):
    return jnp.broadcast_to(a[k : k + 1, :], a.shape)


def inverse_factor(gram):
    lane = lax.broadcasted_iota(jnp.int32, (8, RANK), 1)
    sub = lax.broadcasted_iota(jnp.int32, (8, RANK), 0)
    lanes = lax.broadcasted_iota(jnp.int32, (RANK, RANK), 1)
    rest = gram
    done = []
    for first in range(0, RANK, 8):
        last = first + 8
        panel = rest[first:last, :] if first == 0 else rest[:8, :]
        block = [jnp.broadcast_to(panel[:, first + k : first + k + 1], (8, RANK)) for k in range(8)]
        rows = jnp.where((lane >= first) & (lane < last), jnp.where(lane - first == sub, 1.0, 0.0), panel)
        for k in range(8):
            root = lax.rsqrt(spread_row(block[k], k))
            mult = jnp.where(sub > k, block[k] * (root * root), jnp.where(sub == k, -root, 0.0))
            rows = jnp.where(sub == k, 0.0, rows) - mult * spread_row(rows, k)
            for n in range(k + 1, 8):
                block[n] = block[n] - mult * spread_row(block[n], k)
        done.append(jnp.where(lane < last, rows, 0.0))
        if last < RANK:
            upper = jnp.where(lane >= last, rows, 0.0)
            base = rest[last:, :] if first == 0 else rest[8:, :]
            base = jnp.where((lanes[last:] >= first) & (lanes[last:] < last), 0.0, base)
            change = lax.dot_general(upper, rows, (((0,), (0,)), ((), ())), precision=HIGH, preferred_element_type=F32)
            rest = base - change[last:, :]
    return jnp.concatenate(done, axis=0)


def exchange_kernel(
    momentum_hbm, basis, ortho_out, back_out, scale_out,
    momentum, stage, slots, partial_buf, pair_in, sum_in, projected, gram_buf, gram_x, gram_mid, gram_y, gram_full,
    zq, zx, zmid, zy, back, sq_mine, sq_in,
    load_sem, slot_y_recv, slot_x_recv, slot_send, pair_recv, pair_send, sum_recv, sum_send,
    own_recv, own_send, half_recv, half_send, gx_recv, gx_send, gy_recv, gy_send, ga_recv, ga_send,
    zx_recv, zx_send, zy_recv, zy_send, ty_recv, tx_recv, t_send, sq_recv, sq_send,
):
    f, t = lax.axis_index("fsdp"), lax.axis_index("tensor")
    x, y = f // NY, f % NY
    z, c = t // 2, t % 2
    other = 1 - c

    def at_y(d):
        return (x * NY + (y + d) % NY, t)

    def at_x(d):
        return (((x + d) % NX) * NY + y, t)

    def at_z(d):
        return (f, ((z + d) % NZ) * 2 + c)

    sibling = (f, z * 2 + other)

    def send(src, dst, send_sem, recv_sem, device):
        pltpu.make_async_remote_copy(
            src_ref=src, dst_ref=dst, send_sem=send_sem, recv_sem=recv_sem, device_id=device, device_id_type=MESH
        ).start()

    def wait(ref, sem):
        pltpu.make_async_copy(ref, ref, sem).wait()

    load = pltpu.make_async_copy(momentum_hbm, momentum, load_sem)
    load.start()
    barrier = pltpu.get_barrier_semaphore()
    everyone = [at_y(d) for d in range(1, NY)] + [at_x(d) for d in range(1, NX)]
    everyone += [(f, (t + d) % (2 * NZ)) for d in range(1, 2 * NZ)]
    everyone += [(((x + d) % NX) * NY + y, z * 2 + other) for d in range(1, NX)]
    for device in everyone:
        pl.semaphore_signal(barrier, inc=1, device_id=device, device_id_type=MESH)

    stage[...] = jnp.zeros_like(stage)
    for q in range(4):
        width = min(512, COLS - 512 * q)
        stage[4 * q : 4 * q + 4, :width] = basis[:, 512 * q : 512 * q + width]
    slots[f] = stage[...].astype(BF16)
    pl.semaphore_wait(barrier, len(everyone))

    for d in range(1, NY):
        send(slots.at[f], slots.at[f], slot_send, slot_y_recv.at[d], at_y(d))
    for d in range(1, NX):
        send(slots.at[f], slots.at[f], slot_send, slot_x_recv.at[d], at_x(d))
    for e in range(1, NY):
        source = x * NY + (y - e) % NY
        wait(slots.at[source], slot_y_recv.at[e])
        for d in range(1, NX):
            send(slots.at[source], slots.at[source], slot_send, slot_x_recv.at[d], at_x(d))
    load.wait()
    for d in range(1, NX):
        group = slots.at[pl.ds(((x - d) % NX) * NY, NY)]
        wait(group, slot_x_recv.at[d])

    flat = slots[...].reshape(512, 512)
    to_row = lax.broadcasted_iota(jnp.int32, (RANK, 512), 0)
    from_row = lax.broadcasted_iota(jnp.int32, (RANK, 512), 1)
    total = None
    for q in range(4):
        width = min(512, COLS - 512 * q)
        pick = (from_row == (to_row // 4) * 16 + 4 * q + to_row % 4).astype(F32).astype(BF16)
        part = jnp.dot(pick, flat[:, :width], preferred_element_type=F32).astype(BF16)
        term = lax.dot_general(
            momentum[:, 512 * q : 512 * q + width], part, (((1,), (1,)), ((), ())), preferred_element_type=F32
        )
        total = term if total is None else total + term
    partial_buf[...] = total.reshape(2, ROWS // 2, RANK)

    send(partial_buf.at[other], pair_in, pair_send, pair_recv, sibling)
    wait(pair_in, pair_recv)
    wait(pair_in, pair_send)
    partial_buf[c] = partial_buf[c] + pair_in[...]
    for d in range(1, NZ):
        send(partial_buf.at[c, pl.ds(((z + d) % NZ) * 16, 16)], sum_in.at[d - 1], sum_send, sum_recv, at_z(d))
    wait(sum_in, sum_recv)
    total = partial_buf[c, pl.ds(z * 16, 16), :]
    for d in range(NZ - 1):
        total = total + sum_in[d]
    projected[c, z] = total
    for d in range(1, NZ):
        send(projected.at[c, z], projected.at[c, z], own_send, own_recv.at[d], at_z(d))
    for d in range(1, NZ):
        wait(projected.at[c, (z - d) % NZ], own_recv.at[d])
    send(projected.at[c], projected.at[c], half_send, half_recv, sibling)
    wait(projected.at[other], half_recv)

    proj = projected[...].reshape(ROWS, RANK)
    gram = lax.dot_general(proj, proj, (((0,), (0,)), ((), ())), precision=HIGH, preferred_element_type=F32)
    gram_buf[...] = gram.reshape(8, 16, RANK)
    for d in range(1, NX):
        send(gram_buf.at[2 * ((x + d) % NX) + c], gram_x.at[d - 1], gx_send, gx_recv, at_x(d))

    hi = proj.astype(BF16)
    left = proj - hi.astype(F32)
    mid = left.astype(BF16)
    low = (left - mid.astype(F32)).astype(BF16)
    for piece in range(NX):
        rows = None
        for term in (hi, mid, low):
            product = lax.dot_general(
                momentum[...][:, QUARTER * piece : QUARTER * (piece + 1)], term, (((0,), (0,)), ((), ())),
                preferred_element_type=F32,
            )
            rows = product if rows is None else rows + product
        zq[piece] = rows
    for d in range(1, NX):
        send(zq.at[(x + d) % NX], zx.at[d - 1], zx_send, zx_recv, at_x(d))

    wait(gram_x, gx_recv)
    own = 2 * x + c
    gram_mid[...] = gram_buf[own] + gram_x[0] + gram_x[1] + gram_x[2]
    for d in range(1, NY):
        send(gram_mid, gram_y.at[d - 1], gy_send, gy_recv, at_y(d))
    wait(gram_y, gy_recv)
    total = gram_mid[...]
    for d in range(NY - 1):
        total = total + gram_y[d]
    gram_full[own] = total
    for d in range(NX):
        for core in (c, other):
            if d == 0 and core is c:
                continue
            device = (((x + d) % NX) * NY + y, z * 2 + core)
            send(gram_full.at[own], gram_full.at[own], ga_send, ga_recv, device)
    wait(zx, zx_recv)
    zmid[pl.ds(0, QUARTER), :] = zq[x] + zx[0] + zx[1] + zx[2]
    zmid[pl.ds(QUARTER, NY * SLOT - QUARTER), :] = jnp.zeros((NY * SLOT - QUARTER, RANK), F32)
    for d in range(1, NY):
        send(zmid.at[pl.ds(((y + d) % NY) * SLOT, SLOT)], zy.at[d - 1], zy_send, zy_recv, at_y(d))
    wait(gram_full.at[pl.ds(0, 7)], ga_recv)

    inverse = inverse_factor(gram_full[...].reshape(RANK, RANK))
    ortho = lax.dot_general(proj, inverse, (((1,), (1,)), ((), ())), precision=HIGH, preferred_element_type=F32)
    ortho_out[...] = ortho.astype(BF16)

    wait(zy, zy_recv)
    total = zmid[pl.ds(y * SLOT, SLOT), :]
    for d in range(NY - 1):
        total = total + zy[d]
    mine = lax.dot_general(total, inverse, (((1,), (1,)), ((), ())), precision=HIGH, preferred_element_type=F32)
    back[x, y] = mine.astype(BF16)
    for d in range(1, NY):
        send(back.at[x, y], back.at[x, y], t_send, ty_recv.at[d], at_y(d))
    for d in range(1, NX):
        send(back.at[x, y], back.at[x, y], t_send, tx_recv.at[d], at_x(d))
    for e in range(1, NY):
        source = (y - e) % NY
        wait(back.at[x, source], ty_recv.at[e])
        for d in range(1, NX):
            send(back.at[x, source], back.at[x, source], t_send, tx_recv.at[d], at_x(d))
    for d in range(1, NX):
        wait(back.at[(x - d) % NX], tx_recv.at[d])

    squares = jnp.zeros((8, RANK), F32)
    for piece in range(NX):
        block = back[piece].reshape(NY * SLOT, RANK)[:QUARTER, :]
        back_out[QUARTER * piece : QUARTER * (piece + 1), :] = block
        block = block.astype(F32)
        squares = squares + jnp.sum((block * block).reshape(QUARTER // 8, 8, RANK), axis=0)
    sq_mine[...] = squares
    for d in range(1, 2 * NZ):
        send(sq_mine, sq_in.at[d - 1], sq_send, sq_recv, (f, (t + d) % (2 * NZ)))
    wait(sq_in, sq_recv)
    squares = sq_mine[...] + jnp.sum(sq_in[...], axis=0)
    squares = jnp.sum(squares, axis=0, keepdims=True)
    scale_out[...] = jnp.broadcast_to(lax.rsqrt(squares / FW + 1e-06), (8, RANK))

    wait(slots.at[pl.ds(0, 31)], slot_send)
    wait(sum_in, sum_send)
    wait(sum_in, own_send)
    wait(projected.at[c], half_send)
    wait(gram_x, gx_send)
    wait(gram_y, gy_send)
    wait(gram_full.at[pl.ds(0, 7)], ga_send)
    wait(zx, zx_send)
    wait(zy, zy_send)
    wait(slots.at[pl.ds(0, 31)], t_send)
    wait(sq_in, sq_send)


def update_kernel(momentum, weights, ortho, back, scale, weights_out, momentum_out, basis_out, basis_half):
    f = lax.axis_index("fsdp")

    @pl.when(pl.program_id(0) == 0)
    def _():
        full = back[...].astype(F32) * scale[0:1, :]
        basis_half[...] = full.astype(BF16)
        row = lax.broadcasted_iota(jnp.int32, (8, RANK), 0)
        col = lax.broadcasted_iota(jnp.int32, (8, RANK), 1)
        pick = (col == row + 4 * f).astype(F32)
        own = lax.dot_general(pick, full, (((1,), (1,)), ((), ())), precision=HIGH, preferred_element_type=F32)
        basis_out[...] = own[:4, :]

    q = ortho[...]
    feedback = lax.dot_general(q, back[...], (((1,), (1,)), ((), ())), preferred_element_type=F32)
    momentum_out[...] = (momentum[...].astype(F32) - 0.05 * feedback).astype(BF16)
    update = lax.dot_general(q, basis_half[...], (((1,), (1,)), ((), ())), preferred_element_type=F32)
    weights_out[...] = weights[...] - 0.02 * math.sqrt(DW / RANK) * update


def shards(momentum, weights, basis):
    vmem = pl.BlockSpec(memory_space=pltpu.VMEM)
    dma = pltpu.SemaphoreType.DMA
    ortho, back, scale = pl.pallas_call(
        exchange_kernel,
        out_shape=(
            jax.ShapeDtypeStruct((ROWS, RANK), BF16),
            jax.ShapeDtypeStruct((COLS, RANK), BF16),
            jax.ShapeDtypeStruct((8, RANK), F32),
        ),
        in_specs=[pl.BlockSpec(memory_space=pl.ANY), vmem],
        out_specs=(vmem, vmem, vmem),
        scratch_shapes=[
            pltpu.VMEM((ROWS, COLS), BF16),
            pltpu.VMEM((16, 512), F32),
            pltpu.VMEM((32, 16, 512), BF16),
            pltpu.VMEM((2, ROWS // 2, RANK), F32),
            pltpu.VMEM((ROWS // 2, RANK), F32),
            pltpu.VMEM((NZ - 1, 16, RANK), F32),
            pltpu.VMEM((2, NZ, 16, RANK), F32),
            pltpu.VMEM((8, 16, RANK), F32),
            pltpu.VMEM((NX - 1, 16, RANK), F32),
            pltpu.VMEM((16, RANK), F32),
            pltpu.VMEM((NY - 1, 16, RANK), F32),
            pltpu.VMEM((8, 16, RANK), F32),
            pltpu.VMEM((NX, QUARTER, RANK), F32),
            pltpu.VMEM((NX - 1, QUARTER, RANK), F32),
            pltpu.VMEM((NY * SLOT, RANK), F32),
            pltpu.VMEM((NY - 1, SLOT, RANK), F32),
            pltpu.VMEM((NX, NY, SLOT, RANK), BF16),
            pltpu.VMEM((8, RANK), F32),
            pltpu.VMEM((2 * NZ - 1, 8, RANK), F32),
            dma(()), dma((NY,)), dma((NX,)), dma(()), dma(()), dma(()), dma(()), dma(()),
            dma((NZ,)), dma(()), dma(()), dma(()), dma(()), dma(()), dma(()), dma(()), dma(()), dma(()),
            dma(()), dma(()), dma(()), dma(()), dma((NY,)), dma((NX,)), dma(()), dma(()), dma(()),
        ],
        compiler_params=pltpu.CompilerParams(
            collective_id=0, has_side_effects=True, vmem_limit_bytes=40 * 2**20
        ),
        name="exchange",
    )(momentum, basis.T)
    steps = 4
    block = ROWS // steps
    weights_out, momentum_out, basis_out = pl.pallas_call(
        update_kernel,
        grid=(steps,),
        out_shape=(
            jax.ShapeDtypeStruct((ROWS, COLS), F32),
            jax.ShapeDtypeStruct((ROWS, COLS), BF16),
            jax.ShapeDtypeStruct((4, COLS), F32),
        ),
        in_specs=[
            pl.BlockSpec((block, COLS), lambda i: (i, 0)),
            pl.BlockSpec((block, COLS), lambda i: (i, 0)),
            pl.BlockSpec((block, RANK), lambda i: (i, 0)),
            vmem,
            vmem,
        ],
        out_specs=(
            pl.BlockSpec((block, COLS), lambda i: (i, 0)),
            pl.BlockSpec((block, COLS), lambda i: (i, 0)),
            pl.BlockSpec((4, COLS), lambda i: (0, 0)),
        ),
        scratch_shapes=[pltpu.VMEM((COLS, RANK), BF16)],
        compiler_params=pltpu.CompilerParams(vmem_limit_bytes=40 * 2**20),
        name="update",
    )(momentum, weights, ortho, back, scale)
    return weights_out, momentum_out, basis_out.T


def solution(mesh):
    in_specs = (P("fsdp", "tensor"), P("fsdp", "tensor"), P("tensor", "fsdp"))
    out_specs = (P("fsdp", "tensor"), P("fsdp", "tensor"), P("tensor", "fsdp"))
    return jax.shard_map(shards, mesh=mesh, in_specs=in_specs, out_specs=out_specs, check_vma=False)
```

```python
import functools
import math

import jax
import jax.numpy as jnp
from jax import lax
from jax.experimental import pallas as pl
from jax.experimental.pallas import tpu as pltpu
from jax.sharding import PartitionSpec as P

DW = 8192
FW = 26624
RANK = 128
ROWS = 256
COLS = 1664
NX, NY, NZ = 4, 8, 8
QUARTER = COLS // NX
SLOT = 64
NSLOT = 7
FAR_FIRST = (4, 3, 5, 2, 6, 1, 7)
NEAR_FIRST = (1, 7, 2, 6, 3, 5, 4)

HIGH = lax.Precision.HIGHEST
ACROSS = (((1,), (1,)), ((), ()))
MESH = pl.DeviceIdType.MESH
F32 = jnp.float32
BF16 = jnp.bfloat16


def spread_row(a, k):
    return jnp.broadcast_to(a[k : k + 1, :], a.shape)


def inverse_factor(gram, between):
    lane = lax.broadcasted_iota(jnp.int32, (8, RANK), 1)
    sub = lax.broadcasted_iota(jnp.int32, (8, RANK), 0)
    lanes = lax.broadcasted_iota(jnp.int32, (RANK, RANK), 1)
    rows, coming, rest = gram[0:8], gram[8:16], gram[16:]
    done = []
    for first in range(0, RANK, 8):
        last = first + 8
        more = last < RANK
        inside = (lane >= first) & (lane < last)
        block = [jnp.broadcast_to(rows[:, first + k : first + k + 1], (8, RANK)) for k in range(8)]
        rows = jnp.where(inside, jnp.where(lane - first == sub, 1.0, 0.0), rows)
        if more:
            below = [jnp.broadcast_to(coming[:, first + k : first + k + 1], (8, RANK)) for k in range(8)]
            coming = jnp.where(inside, 0.0, coming)
        pivots = None
        for k in range(8):
            pivot = spread_row(block[k], k)
            inv = 1.0 / pivot
            pivots = pivot if pivots is None else jnp.where(sub == k, pivot, pivots)
            row = spread_row(rows, k)
            mult = jnp.where(sub > k, block[k] * inv, 0.0)
            if more:
                mult_below = below[k] * inv
                coming = coming - mult_below * row
            for n in range(k + 1, 8):
                entry = spread_row(block[n], k)
                block[n] = block[n] - mult * entry
                if more:
                    below[n] = below[n] - mult_below * entry
            rows = rows - mult * row
        rows = rows * lax.rsqrt(pivots)
        done.append(jnp.where(lane < last, rows, 0.0))
        if last + 8 < RANK:
            upper = jnp.where(lane >= last + 8, rows, 0.0)
            base = jnp.where((lanes[last + 8 :] >= first) & (lanes[last + 8 :] < last), 0.0, rest)
            change = lax.dot_general(upper, rows, (((0,), (0,)), ((), ())), precision=HIGH, preferred_element_type=F32)
            rest = base - change[last + 8 :, :]
            rows, coming, rest = coming, rest[:8], rest[8:]
        else:
            rows = coming
        if first // 8 in between:
            between[first // 8]()
    return jnp.concatenate(done, axis=0)


def exchange_kernel(
    momentum_hbm, weights_hbm, basis_hbm, weights_out, momentum_out, basis_out,
    momentum, weights, basis, stage, slots, partial, pair_in, sum_in, projected, gram_buf, gram_x, gram_mid, gram_y, gram_full,
    zq, zx, zmid, zy, back, whole, sq_t, sq_f, sq_t_in, sq_f_in,
    load_sem, weights_sem, basis_sem, slot_y_recv, slot_x_recv, slot_send, pair_recv, pair_send, sum_recv, sum_send,
    own_recv, own_send, half_recv, half_send, gx_recv, gx_send, gy_recv, gy_send, ga_recv, ga_send,
    zx_recv, zx_send, zy_recv, zy_send, ty_recv, tx_recv, t_send, sq_recv, sq_send,
):
    f, t = lax.axis_index("fsdp"), lax.axis_index("tensor")
    x, y = f // NY, f % NY
    z, c = t // 2, t % 2
    other = 1 - c
    pending = []

    def at_y(d):
        return (x * NY + (y + d) % NY, t)

    def at_x(d):
        return (((x + d) % NX) * NY + y, t)

    def at_z(d):
        return (f, ((z + d) % NZ) * 2 + c)

    sibling = (f, z * 2 + other)

    def send(src, dst, send_sem, recv_sem, device):
        pltpu.make_async_remote_copy(
            src_ref=src, dst_ref=dst, send_sem=send_sem, recv_sem=recv_sem, device_id=device, device_id_type=MESH
        ).start()

    def wait(ref, sem):
        pltpu.make_async_copy(ref, ref, sem).wait()

    def later(ref, sem, needed=None):
        pending.append((ref, sem, needed))

    def flush():
        for ref, sem, needed in pending:
            if needed is None:
                wait(ref, sem)
            else:
                pl.when(needed)(functools.partial(wait, ref, sem))

    basis_load = pltpu.make_async_copy(basis_hbm, basis, basis_sem)
    basis_load.start()
    load = pltpu.make_async_copy(momentum_hbm, momentum, load_sem)
    load.start()
    weights_load = pltpu.make_async_copy(weights_hbm, weights, weights_sem)
    weights_load.start()
    barrier = pltpu.get_barrier_semaphore()
    everyone = [at_y(d) for d in range(1, NY)] + [at_x(d) for d in range(1, NX)]
    everyone += [at_z(d) for d in range(1, NZ)] + [sibling]
    for device in everyone:
        pl.semaphore_signal(barrier, inc=1, device_id=device, device_id_type=MESH)

    stage[...] = jnp.zeros_like(stage)
    basis_load.wait()
    for q in range(4):
        width = min(512, COLS - 512 * q)
        stage[4 * q : 4 * q + 4, :width] = basis[:, 512 * q : 512 * q + width]
    slots[f] = stage[...].astype(BF16)
    load.wait()
    weights_load.wait()
    pl.semaphore_wait(barrier, len(everyone))

    for d in FAR_FIRST:
        send(slots.at[f], slots.at[f], slot_send, slot_y_recv.at[d], at_y(d))
    for d in (2, 1, 3):
        send(slots.at[f], slots.at[f], slot_send, slot_x_recv.at[d], at_x(d))
    for e in NEAR_FIRST:
        source = x * NY + (y - e) % NY
        wait(slots.at[source], slot_y_recv.at[e])
        for d in (2, 1, 3):
            send(slots.at[source], slots.at[source], slot_send, slot_x_recv.at[d], at_x(d))
    later(slots.at[pl.ds(0, 31)], slot_send)
    for d in range(1, NX):
        wait(slots.at[pl.ds(((x - d) % NX) * NY, NY)], slot_x_recv.at[d])

    flat = slots[...].reshape(512, 512)
    to_row = lax.broadcasted_iota(jnp.int32, (RANK, 512), 0)
    from_row = lax.broadcasted_iota(jnp.int32, (RANK, 512), 1)
    parts = []
    for q in range(4):
        width = min(512, COLS - 512 * q)
        pick = (from_row == (to_row // 4) * 16 + 4 * q + to_row % 4).astype(F32).astype(BF16)
        parts.append(jnp.dot(pick, flat[:, :width], preferred_element_type=F32).astype(BF16))

    def product(half):
        total = None
        for q in range(4):
            width = min(512, COLS - 512 * q)
            block = momentum[pl.ds(half * (ROWS // 2), ROWS // 2), 512 * q : 512 * q + width]
            term = lax.dot_general(block, parts[q], (((1,), (1,)), ((), ())), preferred_element_type=F32)
            total = term if total is None else total + term
        return total

    partial[other] = product(other)
    for e in FAR_FIRST + (0,):
        rows = pl.ds(((z + e) % NZ) * 16, 16)
        send(partial.at[other, rows], pair_in.at[rows], pair_send, pair_recv.at[e], sibling)
    later(pair_in, pair_send)
    partial[c] = product(c)
    for e in FAR_FIRST:
        rows = pl.ds(((z + e) % NZ) * 16, 16)
        wait(pair_in.at[rows], pair_recv.at[e])
        partial[c, rows, :] = partial[c, rows, :] + pair_in[rows, :]
        send(partial.at[c, rows], sum_in.at[e - 1], sum_send, sum_recv, at_z(e))
    later(sum_in, sum_send)
    rows = pl.ds(z * 16, 16)
    wait(pair_in.at[rows], pair_recv.at[0])
    total = partial[c, rows, :] + pair_in[rows, :]
    wait(sum_in, sum_recv)
    for d in range(NZ - 1):
        total = total + sum_in[d]
    projected[c, z] = total
    for d in FAR_FIRST:
        send(projected.at[c, z], projected.at[c, z], own_send, own_recv.at[d], at_z(d))
    later(sum_in, own_send)
    send(projected.at[c, z], projected.at[c, z], half_send, half_recv, sibling)
    for d in NEAR_FIRST:
        source = (z - d) % NZ
        wait(projected.at[c, source], own_recv.at[d])
        send(projected.at[c, source], projected.at[c, source], half_send, half_recv, sibling)
    wait(projected.at[other], half_recv)
    later(projected.at[c], half_send)

    proj = projected[...].reshape(ROWS, RANK)
    gram = lax.dot_general(proj, proj, (((0,), (0,)), ((), ())), precision=HIGH, preferred_element_type=F32)
    gram_buf[...] = gram.reshape(8, 16, RANK)
    for d in range(1, NX):
        send(gram_buf.at[2 * ((x + d) % NX) + c], gram_x.at[d - 1], gx_send, gx_recv, at_x(d))
    later(gram_x, gx_send)

    hi = proj.astype(BF16)
    left = proj - hi.astype(F32)
    mid = left.astype(BF16)
    low = (left - mid.astype(F32)).astype(BF16)
    terms = jnp.concatenate([hi, mid, low], axis=1)
    for piece in range(NX):
        out = lax.dot_general(
            momentum[:, QUARTER * piece : QUARTER * (piece + 1)], terms, (((0,), (0,)), ((), ())),
            preferred_element_type=F32,
        )
        out = out[:, :RANK] + out[:, RANK : 2 * RANK] + out[:, 2 * RANK :]
        for n in range(NSLOT):
            zq[piece, n, : min(SLOT, QUARTER - n * SLOT), :] = out[n * SLOT : (n + 1) * SLOT, :]
        zq[piece, NSLOT - 1, QUARTER - (NSLOT - 1) * SLOT :, :] = jnp.zeros((NSLOT * SLOT - QUARTER, RANK), F32)

    def send_slot(e):
        slot = (y + e) % NY

        @pl.when(slot < NSLOT)
        def _():
            for d in (2, 1, 3):
                send(zq.at[(x + d) % NX, slot], zx.at[x, slot], zx_send, zx_recv.at[e], at_x(d))

    def reduce_slot(e):
        slot = (y + e) % NY

        @pl.when(slot < NSLOT)
        def _():
            wait(zx.at[pl.ds(0, 3), 0], zx_recv.at[e])
            total = zq[x, slot]
            for d in range(1, NX):
                total = total + zx[(x + d) % NX, slot]
            zmid[slot] = total
            if e:
                send(zmid.at[slot], zy.at[e - 1], zy_send.at[e], zy_recv, at_y(e))

        if e:
            later(zmid.at[0], zy_send.at[e], slot < NSLOT)

    slot_order = FAR_FIRST + (0,)
    for e in slot_order:
        send_slot(e)
    later(zx.at[pl.ds(0, 3)], zx_send)

    wait(gram_x, gx_recv)
    own = 2 * x + c
    gram_mid[...] = gram_buf[own] + gram_x[0] + gram_x[1] + gram_x[2]
    for d in FAR_FIRST:
        send(gram_mid, gram_y.at[d - 1], gy_send, gy_recv, at_y(d))
    later(gram_y, gy_send)
    for e in slot_order[:2]:
        reduce_slot(e)
    wait(gram_y, gy_recv)
    total = gram_mid[...]
    for d in range(NY - 1):
        total = total + gram_y[d]
    gram_full[own] = total
    for d in (2, 1, 3, 0):
        for core in (other, c):
            if d == 0 and core is c:
                continue
            device = (((x + d) % NX) * NY + y, z * 2 + core)
            send(gram_full.at[own], gram_full.at[own], ga_send, ga_recv, device)
    later(gram_full.at[pl.ds(0, 7)], ga_send)
    for e in slot_order[2:5]:
        reduce_slot(e)
    wait(gram_full.at[pl.ds(0, 7)], ga_recv)

    between = {5: functools.partial(reduce_slot, slot_order[5]), 8: functools.partial(reduce_slot, slot_order[6])}
    inverse = inverse_factor(gram_full[...].reshape(RANK, RANK), between)
    reduce_slot(0)
    holder = y < NSLOT

    @pl.when(holder)
    def _():
        wait(zy, zy_recv)
        total = zmid[y]
        for d in range(NY - 1):
            total = total + zy[d]
        mine = lax.dot_general(total, inverse, (((1,), (1,)), ((), ())), precision=HIGH, preferred_element_type=F32)
        mine = mine.astype(BF16)
        back[x, y] = mine
        for d in FAR_FIRST:
            send(back.at[x, y], back.at[x, y], t_send.at[0], ty_recv.at[d], at_y(d))
        for d in (2, 1, 3):
            send(back.at[x, y], back.at[x, y], t_send.at[0], tx_recv.at[d], at_x(d))
        mine = mine.astype(F32)
        sq_t[...] = jnp.sum(mine * mine, axis=0, keepdims=True)

    @pl.when(jnp.logical_not(holder))
    def _():
        sq_t[...] = jnp.zeros_like(sq_t)

    for d in range(1, 2 * NZ):
        send(sq_t, sq_t_in.at[d - 1], sq_send.at[0], sq_recv.at[0], (f, (t + d) % (2 * NZ)))
    later(sq_t_in, sq_send.at[0])
    ortho = lax.dot_general(proj, inverse, (((1,), (1,)), ((), ())), precision=HIGH, preferred_element_type=F32)

    def relay(e):
        source = (y - e) % NY

        @pl.when(source < NSLOT)
        def _():
            wait(back.at[x, source], ty_recv.at[e])
            for d in (2, 1, 3):
                send(back.at[x, source], back.at[x, source], t_send.at[1], tx_recv.at[d], at_x(d))

    for e in NEAR_FIRST[:6]:
        relay(e)
    wait(sq_t_in, sq_recv.at[0])
    sq_f[...] = sq_t[...] + jnp.sum(sq_t_in[...], axis=0)
    for dy in FAR_FIRST + (0,):
        for dx in (2, 1, 3, 0):
            if dx or dy:
                device = (((x + dx) % NX) * NY + (y + dy) % NY, t)
                send(sq_f, sq_f_in.at[dx * NY + dy - 1], sq_send.at[1], sq_recv.at[1], device)
    later(sq_f_in, sq_send.at[1])
    relay(NEAR_FIRST[6])
    later(slots.at[pl.ds(0, 10)], t_send.at[0], holder)
    later(slots.at[pl.ds(0, 18)], t_send.at[1], holder)
    later(slots.at[pl.ds(0, 21)], t_send.at[1], jnp.logical_not(holder))
    def gathered(d):
        piece = (x - d) % NX
        if d:
            wait(back.at[piece], tx_recv.at[d])
        whole[pl.ds(pl.multiple_of(piece * QUARTER, 32), QUARTER), :] = back[piece].reshape(NSLOT * SLOT, RANK)[:QUARTER, :]

    for d in (0, 1, 3, 2):
        gathered(d)
    feedback = lax.dot_general(ortho.astype(BF16), whole[...], ACROSS, preferred_element_type=F32)
    momentum_out[...] = (momentum[...].astype(F32) - 0.05 * feedback).astype(BF16)
    wait(sq_f_in, sq_recv.at[1])
    squares = sq_f[...] + jnp.sum(sq_f_in[...], axis=0)
    scale = lax.rsqrt(squares / FW + 1e-06)
    row = lax.broadcasted_iota(jnp.int32, (16, RANK), 0)
    col = lax.broadcasted_iota(jnp.int32, (16, RANK), 1)
    pick = (col == row + 4 * f) & (row < 4)
    left = jnp.concatenate([ortho * scale, pick.astype(F32)], axis=0).astype(BF16)
    result = lax.dot_general(left, whole[...], ACROSS, preferred_element_type=F32)
    weights_out[...] = weights[...] - 0.02 * math.sqrt(DW / RANK) * result[:ROWS]
    basis_out[...] = result[ROWS : ROWS + 4] * jnp.sum(jnp.where(pick, scale, 0.0), axis=1, keepdims=True)[:4]
    flush()


def place_kernel(weights, momentum, basis, weights_out, momentum_out, basis_out, sems):
    copies = [
        pltpu.make_async_copy(source, target, sems.at[i])
        for i, (source, target) in enumerate(((weights, weights_out), (momentum, momentum_out), (basis, basis_out)))
    ]
    for copy in copies:
        copy.start()
    for copy in copies:
        copy.wait()


def shards(momentum, weights, basis):
    vmem = pl.BlockSpec(memory_space=pltpu.VMEM)
    hbm = pl.BlockSpec(memory_space=pltpu.HBM)
    dma = pltpu.SemaphoreType.DMA
    weights_out, momentum_out, basis_out = pl.pallas_call(
        exchange_kernel,
        out_shape=(
            jax.ShapeDtypeStruct((ROWS, COLS), F32),
            jax.ShapeDtypeStruct((ROWS, COLS), BF16),
            jax.ShapeDtypeStruct((4, COLS), F32),
        ),
        in_specs=[hbm, hbm, hbm],
        out_specs=(vmem, vmem, vmem),
        scratch_shapes=[
            pltpu.VMEM((ROWS, COLS), BF16),
            pltpu.VMEM((ROWS, COLS), F32),
            pltpu.VMEM((4, COLS), F32),
            pltpu.VMEM((16, 512), F32),
            pltpu.VMEM((32, 16, 512), BF16),
            pltpu.VMEM((2, ROWS // 2, RANK), F32),
            pltpu.VMEM((ROWS // 2, RANK), F32),
            pltpu.VMEM((NZ - 1, 16, RANK), F32),
            pltpu.VMEM((2, NZ, 16, RANK), F32),
            pltpu.VMEM((8, 16, RANK), F32),
            pltpu.VMEM((NX - 1, 16, RANK), F32),
            pltpu.VMEM((16, RANK), F32),
            pltpu.VMEM((NY - 1, 16, RANK), F32),
            pltpu.VMEM((8, 16, RANK), F32),
            pltpu.VMEM((NX, NSLOT, SLOT, RANK), F32),
            pltpu.VMEM((NX, NSLOT, SLOT, RANK), F32),
            pltpu.VMEM((NSLOT, SLOT, RANK), F32),
            pltpu.VMEM((NY - 1, SLOT, RANK), F32),
            pltpu.VMEM((NX, NSLOT, SLOT, RANK), BF16),
            pltpu.VMEM((COLS, RANK), BF16),
            pltpu.VMEM((1, RANK), F32),
            pltpu.VMEM((1, RANK), F32),
            pltpu.VMEM((2 * NZ - 1, 1, RANK), F32),
            pltpu.VMEM((NX * NY - 1, 1, RANK), F32),
            dma(()), dma(()), dma(()), dma((NY,)), dma((NX,)), dma(()), dma((NZ,)), dma(()), dma(()), dma(()),
            dma((NZ,)), dma(()), dma(()), dma(()), dma(()), dma(()), dma(()), dma(()), dma(()), dma(()),
            dma((NY,)), dma(()), dma(()), dma((NY,)), dma((NY,)), dma((NX,)), dma((2,)), dma((2,)), dma((2,)),
        ],
        compiler_params=pltpu.CompilerParams(
            collective_id=0, has_side_effects=True, vmem_limit_bytes=48 * 2**20
        ),
        name="exchange",
    )(*[pltpu.with_memory_space_constraint(a, pltpu.HBM) for a in (momentum, weights, basis.T)])
    weights_out, momentum_out, basis_out = pl.pallas_call(
        place_kernel,
        out_shape=(
            jax.ShapeDtypeStruct((ROWS, COLS), F32),
            jax.ShapeDtypeStruct((ROWS, COLS), BF16),
            jax.ShapeDtypeStruct((4, COLS), F32),
        ),
        in_specs=[pl.BlockSpec(memory_space=pl.ANY)] * 3,
        out_specs=(hbm, hbm, hbm),
        scratch_shapes=[dma((3,))],
        compiler_params=pltpu.CompilerParams(vmem_limit_bytes=2 * 2**20),
        name="place",
    )(weights_out, momentum_out, basis_out)
    return weights_out, momentum_out, basis_out.T


def solution(mesh):
    in_specs = (P("fsdp", "tensor"), P("fsdp", "tensor"), P("tensor", "fsdp"))
    out_specs = (P("fsdp", "tensor"), P("fsdp", "tensor"), P("tensor", "fsdp"))
    return jax.shard_map(shards, mesh=mesh, in_specs=in_specs, out_specs=out_specs, check_vma=False)
```

```python
import functools
import math

import jax
import jax.numpy as jnp
from jax import lax
from jax.experimental import pallas as pl
from jax.experimental.pallas import tpu as pltpu
from jax.sharding import PartitionSpec as P

DW = 8192
FW = 26624
RANK = 128
ROWS = 256
COLS = 1664
NX, NY, NZ = 4, 8, 8
QUARTER = COLS // NX
SLOT = 64
AHEAD = 3
NSLOT = 7
FAR_FIRST = (4, 3, 5, 2, 6, 1, 7)
NEAR_FIRST = (1, 7, 2, 6, 3, 5, 4)

HIGH = lax.Precision.HIGHEST
ACROSS = (((1,), (1,)), ((), ()))
MESH = pl.DeviceIdType.MESH
F32 = jnp.float32
BF16 = jnp.bfloat16


def spread_row(a, k):
    return jnp.broadcast_to(a[k : k + 1, :], a.shape)


def inverse_factor(gram):
    lane = lax.broadcasted_iota(jnp.int32, (8, RANK), 1)
    sub = lax.broadcasted_iota(jnp.int32, (8, RANK), 0)
    lanes = lax.broadcasted_iota(jnp.int32, (RANK, RANK), 1)
    panels = [gram[8 * i : 8 * i + 8] for i in range(AHEAD + 1)]
    rest = gram[8 * (AHEAD + 1) :]
    done = []
    for first in range(0, RANK, 8):
        last = first + 8
        inside = (lane >= first) & (lane < last)

        def columns(panel):
            return [jnp.broadcast_to(panel[:, first + k : first + k + 1], (8, RANK)) for k in range(8)]

        block = columns(panels[0])
        below = [columns(panel) for panel in panels[1:]]
        rows = jnp.where(inside, jnp.where(lane - first == sub, 1.0, 0.0), panels[0])
        panels = [jnp.where(inside, 0.0, panel) for panel in panels[1:]]
        pivots = None
        for k in range(8):
            pivot = spread_row(block[k], k)
            inv = 1.0 / pivot
            pivots = pivot if pivots is None else jnp.where(sub == k, pivot, pivots)
            row = spread_row(rows, k)
            mult = jnp.where(sub > k, block[k] * inv, 0.0)
            entries = {n: spread_row(block[n], k) for n in range(k + 1, 8)}
            for n in entries:
                block[n] = block[n] - mult * entries[n]
            rows = rows - mult * row
            for i, column in enumerate(below):
                mult = column[k] * inv
                for n in entries:
                    column[n] = column[n] - mult * entries[n]
                panels[i] = panels[i] - mult * row
        rows = rows * lax.rsqrt(pivots)
        done.append(jnp.where(lane < last, rows, 0.0))
        start = last + 8 * AHEAD
        if start < RANK:
            upper = jnp.where(lane >= start, rows, 0.0)
            base = jnp.where((lanes[start:] >= first) & (lanes[start:] < last), 0.0, rest)
            change = lax.dot_general(upper, rows, (((0,), (0,)), ((), ())), precision=HIGH, preferred_element_type=F32)
            rest = base - change[start:, :]
            panels.append(rest[:8])
            rest = rest[8:]
    return jnp.concatenate(done, axis=0)


def exchange_kernel(
    momentum_hbm, weights_hbm, basis_hbm, weights_out, momentum_out, basis_out,
    momentum, momentum_t, weights, basis, stage, slots, full_basis, partial, pair_in, sum_in, projected, gram_buf, gram_x, gram_mid, gram_y, gram_full,
    zq, zfar, zx, zmid, zy, back, whole, sq_t, sq_f, sq_t_in, sq_f_in,
    load_sem, weights_sem, basis_sem, slot_y_recv, slot_x_recv, slot_send, pair_recv, pair_send, sum_recv, sum_send,
    own_recv, own_send, half_recv, half_send, gx_recv, gx_send, gy_recv, gy_send, ga_recv, ga_send,
    zfar_recv, zx_recv, zx_send, zy_recv, zy_send, ty_recv, tx_recv, t_send, sq_recv, sq_send,
):
    f, t = lax.axis_index("fsdp"), lax.axis_index("tensor")
    x, y = f // NY, f % NY
    z, c = t // 2, t % 2
    other = 1 - c
    pending = []

    def at_y(d):
        return (x * NY + (y + d) % NY, t)

    def at_x(d):
        return (((x + d) % NX) * NY + y, t)

    def at_z(d):
        return (f, ((z + d) % NZ) * 2 + c)

    sibling = (f, z * 2 + other)

    def send(src, dst, send_sem, recv_sem, device):
        pltpu.make_async_remote_copy(
            src_ref=src, dst_ref=dst, send_sem=send_sem, recv_sem=recv_sem, device_id=device, device_id_type=MESH
        ).start()

    def wait(ref, sem):
        pltpu.make_async_copy(ref, ref, sem).wait()

    def later(ref, sem, needed=None):
        pending.append((ref, sem, needed))

    def flush():
        for ref, sem, needed in pending:
            if needed is None:
                wait(ref, sem)
            else:
                pl.when(needed)(functools.partial(wait, ref, sem))

    basis_load = pltpu.make_async_copy(basis_hbm, basis, basis_sem)
    basis_load.start()
    barrier = pltpu.get_barrier_semaphore()
    everyone = [at_y(d) for d in range(1, NY)] + [at_x(d) for d in range(1, NX)]
    everyone += [at_z(d) for d in range(1, NZ)] + [sibling]
    for device in everyone:
        pl.semaphore_signal(barrier, inc=1, device_id=device, device_id_type=MESH)
    load = pltpu.make_async_copy(momentum_hbm, momentum, load_sem)
    load.start()
    weights_load = pltpu.make_async_copy(weights_hbm, weights, weights_sem)
    weights_load.start()

    stage[...] = jnp.zeros_like(stage)
    basis_load.wait()
    for q in range(4):
        width = min(512, COLS - 512 * q)
        stage[4 * q : 4 * q + 4, :width] = basis[:, 512 * q : 512 * q + width]
    slots[f] = stage[...].astype(BF16)
    pl.semaphore_wait(barrier, len(everyone))

    for d in FAR_FIRST:
        send(slots.at[f], slots.at[f], slot_send, slot_y_recv.at[d], at_y(d))
    for d in (2, 1, 3):
        send(slots.at[f], slots.at[f], slot_send, slot_x_recv.at[d], at_x(d))
    for e in NEAR_FIRST:
        source = x * NY + (y - e) % NY
        wait(slots.at[source], slot_y_recv.at[e])
        for d in (2, 1, 3):
            send(slots.at[source], slots.at[source], slot_send, slot_x_recv.at[d], at_x(d))
    later(slots.at[pl.ds(0, 31)], slot_send)
    to_row = lax.broadcasted_iota(jnp.int32, (NY * 4, RANK), 0)
    from_row = lax.broadcasted_iota(jnp.int32, (NY * 4, RANK), 1)

    def arrange(d):
        group = (x - d) % NX
        flat = slots[pl.ds(group * NY, NY)].reshape(RANK, 512)
        for q in range(4):
            width = min(512, COLS - 512 * q)
            pick = (from_row == (to_row // 4) * 16 + 4 * q + to_row % 4).astype(F32).astype(BF16)
            part = jnp.dot(pick, flat[:, :width], preferred_element_type=F32).astype(BF16)
            full_basis[pl.ds(pl.multiple_of(group * NY * 4, 32), NY * 4), 512 * q : 512 * q + width] = part

    arrange(0)
    load.wait()
    for d in (1, 3, 2):
        wait(slots.at[pl.ds(((x - d) % NX) * NY, NY)], slot_x_recv.at[d])
        arrange(d)

    def product(half):
        block = momentum[pl.ds(half * (ROWS // 2), ROWS // 2), :]
        return lax.dot_general(block, full_basis[...], ACROSS, preferred_element_type=F32)

    partial[other] = product(other)
    for e in FAR_FIRST + (0,):
        rows = pl.ds(((z + e) % NZ) * 16, 16)
        send(partial.at[other, rows], pair_in.at[rows], pair_send, pair_recv.at[e], sibling)
    later(pair_in, pair_send)
    partial[c] = product(c)
    for e in FAR_FIRST:
        rows = pl.ds(((z + e) % NZ) * 16, 16)
        wait(pair_in.at[rows], pair_recv.at[e])
        partial[c, rows, :] = partial[c, rows, :] + pair_in[rows, :]
        send(partial.at[c, rows], sum_in.at[e - 1], sum_send, sum_recv, at_z(e))
    later(sum_in, sum_send)
    rows = pl.ds(z * 16, 16)
    wait(pair_in.at[rows], pair_recv.at[0])
    total = partial[c, rows, :] + pair_in[rows, :]
    momentum_t[...] = momentum[...].T
    wait(sum_in, sum_recv)
    for d in range(NZ - 1):
        total = total + sum_in[d]
    projected[c, z] = total
    for d in FAR_FIRST:
        send(projected.at[c, z], projected.at[c, z], own_send, own_recv.at[d], at_z(d))
    later(sum_in, own_send)
    send(projected.at[c, z], projected.at[c, z], half_send, half_recv, sibling)
    for d in NEAR_FIRST:
        source = (z - d) % NZ
        wait(projected.at[c, source], own_recv.at[d])
        send(projected.at[c, source], projected.at[c, source], half_send, half_recv, sibling)
    wait(projected.at[other], half_recv)
    later(projected.at[c], half_send)

    proj = projected[...].reshape(ROWS, RANK)
    gram = lax.dot_general(proj, proj, (((0,), (0,)), ((), ())), precision=HIGH, preferred_element_type=F32)
    gram_buf[...] = gram.reshape(8, 16, RANK)
    for d in range(1, NX):
        send(gram_buf.at[2 * ((x + d) % NX) + c], gram_x.at[d - 1], gx_send, gx_recv, at_x(d))
    later(gram_x, gx_send)

    hi = proj.astype(BF16)
    left = proj - hi.astype(F32)
    mid = left.astype(BF16)
    low = (left - mid.astype(F32)).astype(BF16)
    terms = jnp.concatenate([hi, mid, low], axis=1)
    for piece in range(NX):
        out = jnp.dot(
            momentum_t[QUARTER * piece : QUARTER * (piece + 1), :], terms, preferred_element_type=F32
        )
        out = out[:, :RANK] + out[:, RANK : 2 * RANK] + out[:, 2 * RANK :]
        for n in range(NSLOT):
            zq[piece, n, : min(SLOT, QUARTER - n * SLOT), :] = out[n * SLOT : (n + 1) * SLOT, :]
        zq[piece, NSLOT - 1, QUARTER - (NSLOT - 1) * SLOT :, :] = jnp.zeros((NSLOT * SLOT - QUARTER, RANK), F32)

    def send_slot(e):
        slot = (y + e) % NY
        step = 1 + 2 * (slot % 2)

        @pl.when(slot < NSLOT)
        def _():
            send(zq.at[(x + 2) % NX, slot], zfar.at[e], zx_send.at[0], zfar_recv.at[e], at_x(step))
            send(zq.at[(x + NX - step) % NX, slot], zx.at[0, slot], zx_send.at[1], zx_recv.at[e], at_x(NX - step))

    def pass_slot(e):
        slot = (y + e) % NY
        step = 1 + 2 * (slot % 2)
        target = (x + step) % NX

        @pl.when(slot < NSLOT)
        def _():
            wait(zfar.at[e], zfar_recv.at[e])
            zq[target, slot] = zq[target, slot] + zfar[e]
            send(zq.at[target, slot], zx.at[1, slot], zx_send.at[2], zx_recv.at[e], at_x(step))

    def reduce_slot(e):
        slot = (y + e) % NY

        @pl.when(slot < NSLOT)
        def _():
            wait(zx.at[pl.ds(0, 2), 0], zx_recv.at[e])
            zmid[slot] = zq[x, slot] + zx[0, slot] + zx[1, slot]
            if e:
                send(zmid.at[slot], zy.at[e - 1], zy_send.at[e], zy_recv, at_y(e))

        if e:
            later(zmid.at[0], zy_send.at[e], slot < NSLOT)

    slot_order = FAR_FIRST + (0,)
    for e in slot_order:
        send_slot(e)
    later(zfar.at[pl.ds(0, NSLOT)], zx_send.at[0])
    later(zx.at[0], zx_send.at[1])
    later(zx.at[1], zx_send.at[2])

    wait(gram_x, gx_recv)
    own = 2 * x + c
    gram_mid[...] = gram_buf[own] + gram_x[0] + gram_x[1] + gram_x[2]
    for d in FAR_FIRST:
        send(gram_mid, gram_y.at[d - 1], gy_send, gy_recv, at_y(d))
    later(gram_y, gy_send)
    for e in slot_order:
        pass_slot(e)
    for e in slot_order[:2]:
        reduce_slot(e)
    wait(gram_y, gy_recv)
    total = gram_mid[...]
    for d in range(NY - 1):
        total = total + gram_y[d]
    gram_full[own] = total
    for d in (2, 1, 3, 0):
        for core in (other, c):
            if d == 0 and core is c:
                continue
            device = (((x + d) % NX) * NY + y, z * 2 + core)
            send(gram_full.at[own], gram_full.at[own], ga_send, ga_recv, device)
    later(gram_full.at[pl.ds(0, 7)], ga_send)
    for e in slot_order[2:7]:
        reduce_slot(e)
    wait(gram_full.at[pl.ds(0, 7)], ga_recv)

    inverse = inverse_factor(gram_full[...].reshape(RANK, RANK))
    reduce_slot(0)
    holder = y < NSLOT

    @pl.when(holder)
    def _():
        wait(zy, zy_recv)
        total = zmid[y]
        for d in range(NY - 1):
            total = total + zy[d]
        mine = lax.dot_general(total, inverse, (((1,), (1,)), ((), ())), precision=HIGH, preferred_element_type=F32)
        mine = mine.astype(BF16)
        back[x, y] = mine
        for d in FAR_FIRST:
            send(back.at[x, y], back.at[x, y], t_send.at[0], ty_recv.at[d], at_y(d))
        for d in (2, 1, 3):
            send(back.at[x, y], back.at[x, y], t_send.at[0], tx_recv.at[d], at_x(d))
        mine = mine.astype(F32)
        sq_t[...] = jnp.sum(mine * mine, axis=0, keepdims=True)

    @pl.when(jnp.logical_not(holder))
    def _():
        sq_t[...] = jnp.zeros_like(sq_t)

    for d in range(1, 2 * NZ):
        send(sq_t, sq_t_in.at[d - 1], sq_send.at[0], sq_recv.at[0], (f, (t + d) % (2 * NZ)))
    later(sq_t_in, sq_send.at[0])
    ortho = lax.dot_general(proj, inverse, (((1,), (1,)), ((), ())), precision=HIGH, preferred_element_type=F32)

    def relay(e):
        source = (y - e) % NY

        @pl.when(source < NSLOT)
        def _():
            wait(back.at[x, source], ty_recv.at[e])
            for d in (2, 1, 3):
                send(back.at[x, source], back.at[x, source], t_send.at[1], tx_recv.at[d], at_x(d))

    for e in NEAR_FIRST[:6]:
        relay(e)
    wait(sq_t_in, sq_recv.at[0])
    sq_f[...] = sq_t[...] + jnp.sum(sq_t_in[...], axis=0)
    for dy in FAR_FIRST + (0,):
        for dx in (2, 1, 3, 0):
            if dx or dy:
                device = (((x + dx) % NX) * NY + (y + dy) % NY, t)
                send(sq_f, sq_f_in.at[dx * NY + dy - 1], sq_send.at[1], sq_recv.at[1], device)
    later(sq_f_in, sq_send.at[1])
    relay(NEAR_FIRST[6])
    later(slots.at[pl.ds(0, 10)], t_send.at[0], holder)
    later(slots.at[pl.ds(0, 18)], t_send.at[1], holder)
    later(slots.at[pl.ds(0, 21)], t_send.at[1], jnp.logical_not(holder))
    def gathered(d):
        piece = (x - d) % NX
        if d:
            wait(back.at[piece], tx_recv.at[d])
        whole[pl.ds(pl.multiple_of(piece * QUARTER, 32), QUARTER), :] = back[piece].reshape(NSLOT * SLOT, RANK)[:QUARTER, :]

    for d in (0, 1, 3, 2):
        gathered(d)
    feedback = lax.dot_general(ortho.astype(BF16), whole[...], ACROSS, preferred_element_type=F32)
    momentum_out[...] = (momentum[...].astype(F32) - 0.05 * feedback).astype(BF16)
    weights_load.wait()
    wait(sq_f_in, sq_recv.at[1])
    squares = sq_f[...] + jnp.sum(sq_f_in[...], axis=0)
    scale = lax.rsqrt(squares / FW + 1e-06)
    row = lax.broadcasted_iota(jnp.int32, (16, RANK), 0)
    col = lax.broadcasted_iota(jnp.int32, (16, RANK), 1)
    pick = (col == row + 4 * f) & (row < 4)
    left = jnp.concatenate([ortho * scale, pick.astype(F32)], axis=0).astype(BF16)
    result = lax.dot_general(left, whole[...], ACROSS, preferred_element_type=F32)
    weights_out[...] = weights[...] - 0.02 * math.sqrt(DW / RANK) * result[:ROWS]
    basis_out[...] = result[ROWS : ROWS + 4] * jnp.sum(jnp.where(pick, scale, 0.0), axis=1, keepdims=True)[:4]
    flush()


def place_kernel(weights, momentum, basis, weights_out, momentum_out, basis_out, sems):
    copies = [
        pltpu.make_async_copy(source, target, sems.at[i])
        for i, (source, target) in enumerate(((weights, weights_out), (momentum, momentum_out), (basis, basis_out)))
    ]
    for copy in copies:
        copy.start()
    for copy in copies:
        copy.wait()


def shards(momentum, weights, basis):
    vmem = pl.BlockSpec(memory_space=pltpu.VMEM)
    hbm = pl.BlockSpec(memory_space=pltpu.HBM)
    dma = pltpu.SemaphoreType.DMA
    weights_out, momentum_out, basis_out = pl.pallas_call(
        exchange_kernel,
        out_shape=(
            jax.ShapeDtypeStruct((ROWS, COLS), F32),
            jax.ShapeDtypeStruct((ROWS, COLS), BF16),
            jax.ShapeDtypeStruct((4, COLS), F32),
        ),
        in_specs=[hbm, hbm, hbm],
        out_specs=(vmem, vmem, vmem),
        scratch_shapes=[
            pltpu.VMEM((ROWS, COLS), BF16),
            pltpu.VMEM((COLS, ROWS), BF16),
            pltpu.VMEM((ROWS, COLS), F32),
            pltpu.VMEM((4, COLS), F32),
            pltpu.VMEM((16, 512), F32),
            pltpu.VMEM((32, 16, 512), BF16),
            pltpu.VMEM((RANK, COLS), BF16),
            pltpu.VMEM((2, ROWS // 2, RANK), F32),
            pltpu.VMEM((ROWS // 2, RANK), F32),
            pltpu.VMEM((NZ - 1, 16, RANK), F32),
            pltpu.VMEM((2, NZ, 16, RANK), F32),
            pltpu.VMEM((8, 16, RANK), F32),
            pltpu.VMEM((NX - 1, 16, RANK), F32),
            pltpu.VMEM((16, RANK), F32),
            pltpu.VMEM((NY - 1, 16, RANK), F32),
            pltpu.VMEM((8, 16, RANK), F32),
            pltpu.VMEM((NX, NSLOT, SLOT, RANK), F32),
            pltpu.VMEM((NY, SLOT, RANK), F32),
            pltpu.VMEM((2, NSLOT, SLOT, RANK), F32),
            pltpu.VMEM((NSLOT, SLOT, RANK), F32),
            pltpu.VMEM((NY - 1, SLOT, RANK), F32),
            pltpu.VMEM((NX, NSLOT, SLOT, RANK), BF16),
            pltpu.VMEM((COLS, RANK), BF16),
            pltpu.VMEM((1, RANK), F32),
            pltpu.VMEM((1, RANK), F32),
            pltpu.VMEM((2 * NZ - 1, 1, RANK), F32),
            pltpu.VMEM((NX * NY - 1, 1, RANK), F32),
            dma(()), dma(()), dma(()), dma((NY,)), dma((NX,)), dma(()), dma((NZ,)), dma(()), dma(()), dma(()),
            dma((NZ,)), dma(()), dma(()), dma(()), dma(()), dma(()), dma(()), dma(()), dma(()), dma(()),
            dma((NY,)), dma((NY,)), dma((3,)), dma(()), dma((NY,)), dma((NY,)), dma((NX,)), dma((2,)), dma((2,)), dma((2,)),
        ],
        compiler_params=pltpu.CompilerParams(
            collective_id=0, has_side_effects=True, vmem_limit_bytes=48 * 2**20
        ),
        name="exchange",
    )(*[pltpu.with_memory_space_constraint(a, pltpu.HBM) for a in (momentum, weights, basis.T)])
    weights_out, momentum_out, basis_out = pl.pallas_call(
        place_kernel,
        out_shape=(
            jax.ShapeDtypeStruct((ROWS, COLS), F32),
            jax.ShapeDtypeStruct((ROWS, COLS), BF16),
            jax.ShapeDtypeStruct((4, COLS), F32),
        ),
        in_specs=[pl.BlockSpec(memory_space=pl.ANY)] * 3,
        out_specs=(hbm, hbm, hbm),
        scratch_shapes=[dma((3,))],
        compiler_params=pltpu.CompilerParams(vmem_limit_bytes=2 * 2**20),
        name="place",
    )(weights_out, momentum_out, basis_out)
    return weights_out, momentum_out, basis_out.T


def solution(mesh):
    in_specs = (P("fsdp", "tensor"), P("fsdp", "tensor"), P("tensor", "fsdp"))
    out_specs = (P("fsdp", "tensor"), P("fsdp", "tensor"), P("tensor", "fsdp"))
    return jax.shard_map(shards, mesh=mesh, in_specs=in_specs, out_specs=out_specs, check_vma=False)
```

```python
import functools
import math

import jax
import jax.numpy as jnp
from jax import lax
from jax.experimental import pallas as pl
from jax.experimental.pallas import tpu as pltpu
from jax.sharding import PartitionSpec as P

DW = 8192
FW = 26624
RANK = 128
ROWS = 256
COLS = 1664
NX, NY, NZ = 4, 8, 8
QUARTER = COLS // NX
SLOT = 64
AHEAD = 3
NSLOT = 7
FAR_FIRST = (4, 3, 5, 2, 6, 1, 7)
NEAR_FIRST = (1, 7, 2, 6, 3, 5, 4)

HIGH = lax.Precision.HIGHEST
ACROSS = (((1,), (1,)), ((), ()))
MESH = pl.DeviceIdType.MESH
F32 = jnp.float32
BF16 = jnp.bfloat16


def spread_row(a, k):
    return jnp.broadcast_to(a[k : k + 1, :], a.shape)


def inverse_factor(gram):
    lane = lax.broadcasted_iota(jnp.int32, (8, RANK), 1)
    sub = lax.broadcasted_iota(jnp.int32, (8, RANK), 0)
    lanes = lax.broadcasted_iota(jnp.int32, (RANK, RANK), 1)
    panels = [gram[8 * i : 8 * i + 8] for i in range(AHEAD + 1)]
    rest = gram[8 * (AHEAD + 1) :]
    done = []
    for first in range(0, RANK, 8):
        last = first + 8
        inside = (lane >= first) & (lane < last)

        def columns(panel):
            return [jnp.broadcast_to(panel[:, first + k : first + k + 1], (8, RANK)) for k in range(8)]

        block = columns(panels[0])
        below = [columns(panel) for panel in panels[1:]]
        rows = jnp.where(inside, jnp.where(lane - first == sub, 1.0, 0.0), panels[0])
        panels = [jnp.where(inside, 0.0, panel) for panel in panels[1:]]
        pivots = None
        for k in range(8):
            pivot = spread_row(block[k], k)
            inv = 1.0 / pivot
            pivots = pivot if pivots is None else jnp.where(sub == k, pivot, pivots)
            row = spread_row(rows, k)
            mult = jnp.where(sub > k, block[k] * inv, 0.0)
            entries = {n: spread_row(block[n], k) for n in range(k + 1, 8)}
            for n in entries:
                block[n] = block[n] - mult * entries[n]
            rows = rows - mult * row
            for i, column in enumerate(below):
                mult = column[k] * inv
                for n in entries:
                    column[n] = column[n] - mult * entries[n]
                panels[i] = panels[i] - mult * row
        rows = rows * lax.rsqrt(pivots)
        done.append(jnp.where(lane < last, rows, 0.0))
        start = last + 8 * AHEAD
        if start < RANK:
            upper = jnp.where(lane >= start, rows, 0.0)
            base = jnp.where((lanes[start:] >= first) & (lanes[start:] < last), 0.0, rest)
            change = lax.dot_general(upper, rows, (((0,), (0,)), ((), ())), precision=HIGH, preferred_element_type=F32)
            rest = base - change[start:, :]
            panels.append(rest[:8])
            rest = rest[8:]
    return jnp.concatenate(done, axis=0)


def exchange_kernel(
    momentum_hbm, weights_hbm, basis_hbm, weights_out, momentum_out, basis_out,
    momentum, momentum_t, weights, basis, stage, slots, full_basis, partial, pair_in, sum_in, projected, gram_buf, gram_x, gram_mid, gram_y, gram_full,
    zq, zfar, zx, zmid, zy, back, whole, sq_t, sq_f, sq_t_in, sq_f_in,
    load_sem, weights_sem, basis_sem, slot_y_recv, slot_x_recv, slot_send, pair_recv, pair_send, sum_recv, sum_send,
    own_recv, own_send, half_recv, half_send, gx_recv, gx_send, gy_recv, gy_send, ga_recv, ga_send,
    zfar_recv, zx_recv, zx_send, zy_recv, zy_send, ty_recv, tx_recv, t_send, sq_recv, sq_send,
):
    f, t = lax.axis_index("fsdp"), lax.axis_index("tensor")
    x, y = f // NY, f % NY
    z, c = t // 2, t % 2
    other = 1 - c
    pending = []

    def at_y(d):
        return (x * NY + (y + d) % NY, t)

    def at_x(d):
        return (((x + d) % NX) * NY + y, t)

    def at_z(d):
        return (f, ((z + d) % NZ) * 2 + c)

    sibling = (f, z * 2 + other)

    def send(src, dst, send_sem, recv_sem, device):
        pltpu.make_async_remote_copy(
            src_ref=src, dst_ref=dst, send_sem=send_sem, recv_sem=recv_sem, device_id=device, device_id_type=MESH
        ).start()

    def wait(ref, sem):
        pltpu.make_async_copy(ref, ref, sem).wait()

    def later(ref, sem, needed=None):
        pending.append((ref, sem, needed))

    def flush():
        for ref, sem, needed in pending:
            if needed is None:
                wait(ref, sem)
            else:
                pl.when(needed)(functools.partial(wait, ref, sem))

    basis_load = pltpu.make_async_copy(basis_hbm, basis, basis_sem)
    basis_load.start()
    barrier = pltpu.get_barrier_semaphore()
    everyone = [at(d) for d in FAR_FIRST for at in (at_y, at_z)] + [at_x(d) for d in (2, 1, 3)] + [sibling]
    for device in everyone:
        pl.semaphore_signal(barrier, inc=1, device_id=device, device_id_type=MESH)
    load = pltpu.make_async_copy(momentum_hbm, momentum, load_sem)
    load.start()
    weights_load = pltpu.make_async_copy(weights_hbm, weights, weights_sem)
    weights_load.start()

    stage[...] = jnp.zeros_like(stage)
    basis_load.wait()
    for q in range(4):
        width = min(512, COLS - 512 * q)
        stage[4 * q : 4 * q + 4, :width] = basis[:, 512 * q : 512 * q + width]
    slots[f] = stage[...].astype(BF16)
    pl.semaphore_wait(barrier, len(everyone))

    for d in (2, 1, 3):
        send(slots.at[f], slots.at[f], slot_send, slot_x_recv.at[d], at_x(d))
    for d in NEAR_FIRST:
        send(slots.at[f], slots.at[f], slot_send, slot_y_recv.at[d], at_y(d))
    for e in NEAR_FIRST:
        source = x * NY + (y - e) % NY
        wait(slots.at[source], slot_y_recv.at[e])
        for d in (2, 1, 3):
            send(slots.at[source], slots.at[source], slot_send, slot_x_recv.at[d], at_x(d))
    later(slots.at[pl.ds(0, 31)], slot_send)
    to_row = lax.broadcasted_iota(jnp.int32, (NY * 4, RANK), 0)
    from_row = lax.broadcasted_iota(jnp.int32, (NY * 4, RANK), 1)

    def arrange(d):
        group = (x - d) % NX
        flat = slots[pl.ds(group * NY, NY)].reshape(RANK, 512)
        for q in range(4):
            width = min(512, COLS - 512 * q)
            pick = (from_row == (to_row // 4) * 16 + 4 * q + to_row % 4).astype(F32).astype(BF16)
            part = jnp.dot(pick, flat[:, :width], preferred_element_type=F32).astype(BF16)
            full_basis[pl.ds(pl.multiple_of(group * NY * 4, 32), NY * 4), 512 * q : 512 * q + width] = part

    arrange(0)
    load.wait()
    for d in (1, 3, 2):
        wait(slots.at[pl.ds(((x - d) % NX) * NY, NY)], slot_x_recv.at[d])
        arrange(d)

    def product(half):
        block = momentum[pl.ds(half * (ROWS // 2), ROWS // 2), :]
        return lax.dot_general(block, full_basis[...], ACROSS, preferred_element_type=F32)

    partial[other] = product(other)
    for e in FAR_FIRST + (0,):
        rows = pl.ds(((z + e) % NZ) * 16, 16)
        send(partial.at[other, rows], pair_in.at[rows], pair_send, pair_recv.at[e], sibling)
    later(pair_in, pair_send)
    partial[c] = product(c)
    for e in FAR_FIRST:
        rows = pl.ds(((z + e) % NZ) * 16, 16)
        wait(pair_in.at[rows], pair_recv.at[e])
        partial[c, rows, :] = partial[c, rows, :] + pair_in[rows, :]
        send(partial.at[c, rows], sum_in.at[e - 1], sum_send, sum_recv, at_z(e))
    later(sum_in, sum_send)
    rows = pl.ds(z * 16, 16)
    wait(pair_in.at[rows], pair_recv.at[0])
    total = partial[c, rows, :] + pair_in[rows, :]
    momentum_t[...] = momentum[...].T
    wait(sum_in, sum_recv)
    for d in range(NZ - 1):
        total = total + sum_in[d]
    projected[c, z] = total
    for d in FAR_FIRST:
        send(projected.at[c, z], projected.at[c, z], own_send, own_recv.at[d], at_z(d))
    later(sum_in, own_send)
    send(projected.at[c, z], projected.at[c, z], half_send, half_recv, sibling)
    for d in NEAR_FIRST:
        source = (z - d) % NZ
        wait(projected.at[c, source], own_recv.at[d])
        send(projected.at[c, source], projected.at[c, source], half_send, half_recv, sibling)
    wait(projected.at[other], half_recv)
    later(projected.at[c], half_send)

    proj = projected[...].reshape(ROWS, RANK)
    gram = lax.dot_general(proj, proj, (((0,), (0,)), ((), ())), precision=HIGH, preferred_element_type=F32)
    gram_buf[...] = gram.reshape(8, 16, RANK)
    for d in range(1, NX):
        send(gram_buf.at[2 * ((x + d) % NX) + c], gram_x.at[d - 1], gx_send, gx_recv, at_x(d))
    later(gram_x, gx_send)

    hi = proj.astype(BF16)
    left = proj - hi.astype(F32)
    mid = left.astype(BF16)
    low = (left - mid.astype(F32)).astype(BF16)
    terms = jnp.concatenate([hi, mid, low], axis=1)
    for piece in range(NX):
        out = jnp.dot(
            momentum_t[QUARTER * piece : QUARTER * (piece + 1), :], terms, preferred_element_type=F32
        )
        out = out[:, :RANK] + out[:, RANK : 2 * RANK] + out[:, 2 * RANK :]
        for n in range(NSLOT):
            zq[piece, n, : min(SLOT, QUARTER - n * SLOT), :] = out[n * SLOT : (n + 1) * SLOT, :]
        zq[piece, NSLOT - 1, QUARTER - (NSLOT - 1) * SLOT :, :] = jnp.zeros((NSLOT * SLOT - QUARTER, RANK), F32)

    def send_slot(e):
        slot = (y + e) % NY
        step = 1 + 2 * (slot % 2)

        @pl.when(slot < NSLOT)
        def _():
            send(zq.at[(x + 2) % NX, slot], zfar.at[e], zx_send.at[0], zfar_recv.at[e], at_x(step))
            send(zq.at[(x + NX - step) % NX, slot], zx.at[0, slot], zx_send.at[1], zx_recv.at[e], at_x(NX - step))

    def pass_slot(e):
        slot = (y + e) % NY
        step = 1 + 2 * (slot % 2)
        target = (x + step) % NX

        @pl.when(slot < NSLOT)
        def _():
            wait(zfar.at[e], zfar_recv.at[e])
            zq[target, slot] = zq[target, slot] + zfar[e]
            send(zq.at[target, slot], zx.at[1, slot], zx_send.at[2], zx_recv.at[e], at_x(step))

    def reduce_slot(e):
        slot = (y + e) % NY

        @pl.when(slot < NSLOT)
        def _():
            wait(zx.at[pl.ds(0, 2), 0], zx_recv.at[e])
            zmid[slot] = zq[x, slot] + zx[0, slot] + zx[1, slot]
            if e:
                send(zmid.at[slot], zy.at[e - 1], zy_send.at[e], zy_recv, at_y(e))

        if e:
            later(zmid.at[0], zy_send.at[e], slot < NSLOT)

    slot_order = FAR_FIRST + (0,)
    for e in slot_order:
        send_slot(e)
    later(zfar.at[pl.ds(0, NSLOT)], zx_send.at[0])
    later(zx.at[0], zx_send.at[1])
    later(zx.at[1], zx_send.at[2])

    wait(gram_x, gx_recv)
    own = 2 * x + c
    gram_mid[...] = gram_buf[own] + gram_x[0] + gram_x[1] + gram_x[2]
    for d in FAR_FIRST:
        send(gram_mid, gram_y.at[d - 1], gy_send, gy_recv, at_y(d))
    later(gram_y, gy_send)
    for e in slot_order:
        pass_slot(e)
    for e in slot_order[:2]:
        reduce_slot(e)
    wait(gram_y, gy_recv)
    total = gram_mid[...]
    for d in range(NY - 1):
        total = total + gram_y[d]
    gram_full[own] = total
    for d in (2, 1, 3, 0):
        for core in (other, c):
            if d == 0 and core is c:
                continue
            device = (((x + d) % NX) * NY + y, z * 2 + core)
            send(gram_full.at[own], gram_full.at[own], ga_send, ga_recv, device)
    later(gram_full.at[pl.ds(0, 7)], ga_send)
    for e in slot_order[2:7]:
        reduce_slot(e)
    wait(gram_full.at[pl.ds(0, 7)], ga_recv)

    inverse = inverse_factor(gram_full[...].reshape(RANK, RANK))
    reduce_slot(0)
    holder = y < NSLOT

    @pl.when(holder)
    def _():
        wait(zy, zy_recv)
        total = zmid[y]
        for d in range(NY - 1):
            total = total + zy[d]
        mine = lax.dot_general(total, inverse, (((1,), (1,)), ((), ())), precision=HIGH, preferred_element_type=F32)
        mine = mine.astype(BF16)
        back[x, y] = mine
        for d in (2, 1, 3):
            send(back.at[x, y], back.at[x, y], t_send.at[0], tx_recv.at[d], at_x(d))
        for d in NEAR_FIRST:
            send(back.at[x, y], back.at[x, y], t_send.at[0], ty_recv.at[d], at_y(d))
        mine = mine.astype(F32)
        sq_t[...] = jnp.sum(mine * mine, axis=0, keepdims=True)

    @pl.when(jnp.logical_not(holder))
    def _():
        sq_t[...] = jnp.zeros_like(sq_t)

    for d in range(1, 2 * NZ):
        send(sq_t, sq_t_in.at[d - 1], sq_send.at[0], sq_recv.at[0], (f, (t + d) % (2 * NZ)))
    later(sq_t_in, sq_send.at[0])
    ortho = lax.dot_general(proj, inverse, (((1,), (1,)), ((), ())), precision=HIGH, preferred_element_type=F32)

    def relay(e):
        source = (y - e) % NY

        @pl.when(source < NSLOT)
        def _():
            wait(back.at[x, source], ty_recv.at[e])
            for d in (2, 1, 3):
                send(back.at[x, source], back.at[x, source], t_send.at[1], tx_recv.at[d], at_x(d))

    for e in NEAR_FIRST[:6]:
        relay(e)
    wait(sq_t_in, sq_recv.at[0])
    sq_f[...] = sq_t[...] + jnp.sum(sq_t_in[...], axis=0)
    for dy in FAR_FIRST + (0,):
        for dx in (2, 1, 3, 0):
            if dx or dy:
                device = (((x + dx) % NX) * NY + (y + dy) % NY, t)
                send(sq_f, sq_f_in.at[dx * NY + dy - 1], sq_send.at[1], sq_recv.at[1], device)
    later(sq_f_in, sq_send.at[1])
    relay(NEAR_FIRST[6])
    later(slots.at[pl.ds(0, 10)], t_send.at[0], holder)
    later(slots.at[pl.ds(0, 18)], t_send.at[1], holder)
    later(slots.at[pl.ds(0, 21)], t_send.at[1], jnp.logical_not(holder))
    def gathered(d):
        piece = (x - d) % NX
        if d:
            wait(back.at[piece], tx_recv.at[d])
        whole[pl.ds(pl.multiple_of(piece * QUARTER, 32), QUARTER), :] = back[piece].reshape(NSLOT * SLOT, RANK)[:QUARTER, :]

    for d in (0, 1, 3, 2):
        gathered(d)
    feedback = lax.dot_general(ortho.astype(BF16), whole[...], ACROSS, preferred_element_type=F32)
    momentum_out[...] = (momentum[...].astype(F32) - 0.05 * feedback).astype(BF16)
    weights_load.wait()
    wait(sq_f_in, sq_recv.at[1])
    squares = sq_f[...] + jnp.sum(sq_f_in[...], axis=0)
    scale = lax.rsqrt(squares / FW + 1e-06)
    row = lax.broadcasted_iota(jnp.int32, (16, RANK), 0)
    col = lax.broadcasted_iota(jnp.int32, (16, RANK), 1)
    pick = (col == row + 4 * f) & (row < 4)
    left = jnp.concatenate([ortho * scale, pick.astype(F32)], axis=0).astype(BF16)
    result = lax.dot_general(left, whole[...], ACROSS, preferred_element_type=F32)
    weights_out[...] = weights[...] - 0.02 * math.sqrt(DW / RANK) * result[:ROWS]
    basis_out[...] = result[ROWS : ROWS + 4] * jnp.sum(jnp.where(pick, scale, 0.0), axis=1, keepdims=True)[:4]
    flush()


def place_kernel(weights, momentum, basis, weights_out, momentum_out, basis_out, sems):
    copies = [
        pltpu.make_async_copy(source, target, sems.at[i])
        for i, (source, target) in enumerate(((weights, weights_out), (momentum, momentum_out), (basis, basis_out)))
    ]
    for copy in copies:
        copy.start()
    for copy in copies:
        copy.wait()


def shards(momentum, weights, basis):
    vmem = pl.BlockSpec(memory_space=pltpu.VMEM)
    hbm = pl.BlockSpec(memory_space=pltpu.HBM)
    dma = pltpu.SemaphoreType.DMA
    weights_out, momentum_out, basis_out = pl.pallas_call(
        exchange_kernel,
        out_shape=(
            jax.ShapeDtypeStruct((ROWS, COLS), F32),
            jax.ShapeDtypeStruct((ROWS, COLS), BF16),
            jax.ShapeDtypeStruct((4, COLS), F32),
        ),
        in_specs=[hbm, hbm, hbm],
        out_specs=(vmem, vmem, vmem),
        scratch_shapes=[
            pltpu.VMEM((ROWS, COLS), BF16),
            pltpu.VMEM((COLS, ROWS), BF16),
            pltpu.VMEM((ROWS, COLS), F32),
            pltpu.VMEM((4, COLS), F32),
            pltpu.VMEM((16, 512), F32),
            pltpu.VMEM((32, 16, 512), BF16),
            pltpu.VMEM((RANK, COLS), BF16),
            pltpu.VMEM((2, ROWS // 2, RANK), F32),
            pltpu.VMEM((ROWS // 2, RANK), F32),
            pltpu.VMEM((NZ - 1, 16, RANK), F32),
            pltpu.VMEM((2, NZ, 16, RANK), F32),
            pltpu.VMEM((8, 16, RANK), F32),
            pltpu.VMEM((NX - 1, 16, RANK), F32),
            pltpu.VMEM((16, RANK), F32),
            pltpu.VMEM((NY - 1, 16, RANK), F32),
            pltpu.VMEM((8, 16, RANK), F32),
            pltpu.VMEM((NX, NSLOT, SLOT, RANK), F32),
            pltpu.VMEM((NY, SLOT, RANK), F32),
            pltpu.VMEM((2, NSLOT, SLOT, RANK), F32),
            pltpu.VMEM((NSLOT, SLOT, RANK), F32),
            pltpu.VMEM((NY - 1, SLOT, RANK), F32),
            pltpu.VMEM((NX, NSLOT, SLOT, RANK), BF16),
            pltpu.VMEM((COLS, RANK), BF16),
            pltpu.VMEM((1, RANK), F32),
            pltpu.VMEM((1, RANK), F32),
            pltpu.VMEM((2 * NZ - 1, 1, RANK), F32),
            pltpu.VMEM((NX * NY - 1, 1, RANK), F32),
            dma(()), dma(()), dma(()), dma((NY,)), dma((NX,)), dma(()), dma((NZ,)), dma(()), dma(()), dma(()),
            dma((NZ,)), dma(()), dma(()), dma(()), dma(()), dma(()), dma(()), dma(()), dma(()), dma(()),
            dma((NY,)), dma((NY,)), dma((3,)), dma(()), dma((NY,)), dma((NY,)), dma((NX,)), dma((2,)), dma((2,)), dma((2,)),
        ],
        compiler_params=pltpu.CompilerParams(
            collective_id=0, has_side_effects=True, vmem_limit_bytes=48 * 2**20
        ),
        name="exchange",
    )(*[pltpu.with_memory_space_constraint(a, pltpu.HBM) for a in (momentum, weights, basis.T)])
    weights_out, momentum_out, basis_out = pl.pallas_call(
        place_kernel,
        out_shape=(
            jax.ShapeDtypeStruct((ROWS, COLS), F32),
            jax.ShapeDtypeStruct((ROWS, COLS), BF16),
            jax.ShapeDtypeStruct((4, COLS), F32),
        ),
        in_specs=[pl.BlockSpec(memory_space=pl.ANY)] * 3,
        out_specs=(hbm, hbm, hbm),
        scratch_shapes=[dma((3,))],
        compiler_params=pltpu.CompilerParams(vmem_limit_bytes=2 * 2**20),
        name="place",
    )(weights_out, momentum_out, basis_out)
    return weights_out, momentum_out, basis_out.T


def solution(mesh):
    in_specs = (P("fsdp", "tensor"), P("fsdp", "tensor"), P("tensor", "fsdp"))
    out_specs = (P("fsdp", "tensor"), P("fsdp", "tensor"), P("tensor", "fsdp"))
    return jax.shard_map(shards, mesh=mesh, in_specs=in_specs, out_specs=out_specs, check_vma=False)
```

```python
import functools
import math

import jax
import jax.numpy as jnp
from jax import lax
from jax.experimental import pallas as pl
from jax.experimental.pallas import tpu as pltpu
from jax.sharding import PartitionSpec as P

DW = 8192
FW = 26624
RANK = 128
ROWS = 256
COLS = 1664
NX, NY, NZ = 4, 8, 8
QUARTER = COLS // NX
SLOT = 64
AHEAD = 3
NSLOT = 7
FAR_FIRST = (4, 3, 5, 2, 6, 1, 7)
NEAR_FIRST = (1, 7, 2, 6, 3, 5, 4)

HIGH = lax.Precision.HIGHEST
ACROSS = (((1,), (1,)), ((), ()))
MESH = pl.DeviceIdType.MESH
F32 = jnp.float32
BF16 = jnp.bfloat16


def spread_row(a, k):
    return jnp.broadcast_to(a[k : k + 1, :], a.shape)


def inverse_factor(gram):
    lane = lax.broadcasted_iota(jnp.int32, (8, RANK), 1)
    sub = lax.broadcasted_iota(jnp.int32, (8, RANK), 0)
    lanes = lax.broadcasted_iota(jnp.int32, (RANK, RANK), 1)
    panels = [gram[8 * i : 8 * i + 8] for i in range(AHEAD + 1)]
    rest = gram[8 * (AHEAD + 1) :]
    done = []
    for first in range(0, RANK, 8):
        last = first + 8
        inside = (lane >= first) & (lane < last)

        def columns(panel):
            return [jnp.broadcast_to(panel[:, first + k : first + k + 1], (8, RANK)) for k in range(8)]

        block = columns(panels[0])
        below = [columns(panel) for panel in panels[1:]]
        rows = jnp.where(inside, jnp.where(lane - first == sub, 1.0, 0.0), panels[0])
        panels = [jnp.where(inside, 0.0, panel) for panel in panels[1:]]
        pivots = None
        for k in range(8):
            pivot = spread_row(block[k], k)
            inv = 1.0 / pivot
            pivots = pivot if pivots is None else jnp.where(sub == k, pivot, pivots)
            row = spread_row(rows, k)
            mult = jnp.where(sub > k, block[k] * inv, 0.0)
            entries = {n: spread_row(block[n], k) for n in range(k + 1, 8)}
            for n in entries:
                block[n] = block[n] - mult * entries[n]
            rows = rows - mult * row
            for i, column in enumerate(below):
                mult = column[k] * inv
                for n in entries:
                    column[n] = column[n] - mult * entries[n]
                panels[i] = panels[i] - mult * row
        rows = rows * lax.rsqrt(pivots)
        done.append(jnp.where(lane < last, rows, 0.0))
        start = last + 8 * AHEAD
        if start < RANK:
            upper = jnp.where(lane >= start, rows, 0.0)
            base = jnp.where((lanes[start:] >= first) & (lanes[start:] < last), 0.0, rest)
            change = lax.dot_general(upper, rows, (((0,), (0,)), ((), ())), precision=HIGH, preferred_element_type=F32)
            rest = base - change[start:, :]
            panels.append(rest[:8])
            rest = rest[8:]
    return jnp.concatenate(done, axis=0)


def exchange_kernel(
    momentum_hbm, weights_hbm, basis_hbm, weights_out, momentum_out, basis_out,
    momentum, momentum_t, weights, basis, stage, slots, full_basis, partial, pair_in, sum_in, projected, gram_buf, gram_x, gram_mid, gram_y, gram_full,
    zq, zfar, zx, zmid, zy, back, whole, sq_t, sq_f, sq_t_in, sq_f_in,
    load_sem, weights_sem, basis_sem, slot_y_recv, slot_x_recv, slot_send, pair_recv, pair_send, sum_recv, sum_send,
    own_recv, own_send, half_recv, half_send, gx_recv, gx_send, gy_recv, gy_send, ga_recv, ga_send,
    zfar_recv, zx_recv, zx_send, zy_recv, zy_send, ty_recv, tx_recv, t_send, sq_recv, sq_send,
):
    f, t = lax.axis_index("fsdp"), lax.axis_index("tensor")
    x, y = f // NY, f % NY
    z, c = t // 2, t % 2
    other = 1 - c
    pending = []

    def at_y(d):
        return (x * NY + (y + d) % NY, t)

    def at_x(d):
        return (((x + d) % NX) * NY + y, t)

    def at_z(d):
        return (f, ((z + d) % NZ) * 2 + c)

    sibling = (f, z * 2 + other)

    def send(src, dst, send_sem, recv_sem, device):
        pltpu.make_async_remote_copy(
            src_ref=src, dst_ref=dst, send_sem=send_sem, recv_sem=recv_sem, device_id=device, device_id_type=MESH
        ).start()

    def wait(ref, sem):
        pltpu.make_async_copy(ref, ref, sem).wait()

    def later(ref, sem, needed=None):
        pending.append((ref, sem, needed))

    def flush():
        for ref, sem, needed in pending:
            if needed is None:
                wait(ref, sem)
            else:
                pl.when(needed)(functools.partial(wait, ref, sem))

    basis_load = pltpu.make_async_copy(basis_hbm, basis, basis_sem)
    basis_load.start()
    barrier = pltpu.get_barrier_semaphore()
    everyone = [at(d) for d in FAR_FIRST for at in (at_y, at_z)] + [at_x(d) for d in (2, 1, 3)] + [sibling]
    for device in everyone:
        pl.semaphore_signal(barrier, inc=1, device_id=device, device_id_type=MESH)
    load = pltpu.make_async_copy(momentum_hbm, momentum, load_sem)
    load.start()
    weights_load = pltpu.make_async_copy(weights_hbm, weights, weights_sem)
    weights_load.start()

    stage[...] = jnp.zeros_like(stage)
    basis_load.wait()
    for q in range(4):
        width = min(512, COLS - 512 * q)
        stage[4 * q : 4 * q + 4, :width] = basis[:, 512 * q : 512 * q + width]
    slots[f] = stage[...].astype(BF16)
    pl.semaphore_wait(barrier, len(everyone))

    for d in (2, 1, 3):
        send(slots.at[f], slots.at[f], slot_send, slot_x_recv.at[d], at_x(d))
    for d in NEAR_FIRST:
        send(slots.at[f], slots.at[f], slot_send, slot_y_recv.at[d], at_y(d))
    for e in NEAR_FIRST:
        source = x * NY + (y - e) % NY
        wait(slots.at[source], slot_y_recv.at[e])
        for d in (2, 1, 3):
            send(slots.at[source], slots.at[source], slot_send, slot_x_recv.at[d], at_x(d))
    later(slots.at[pl.ds(0, 31)], slot_send)
    to_row = lax.broadcasted_iota(jnp.int32, (NY * 4, RANK), 0)
    from_row = lax.broadcasted_iota(jnp.int32, (NY * 4, RANK), 1)

    def arrange(d):
        group = (x - d) % NX
        flat = slots[pl.ds(group * NY, NY)].reshape(RANK, 512)
        for q in range(4):
            width = min(512, COLS - 512 * q)
            pick = (from_row == (to_row // 4) * 16 + 4 * q + to_row % 4).astype(F32).astype(BF16)
            part = jnp.dot(pick, flat[:, :width], preferred_element_type=F32).astype(BF16)
            full_basis[pl.ds(pl.multiple_of(group * NY * 4, 32), NY * 4), 512 * q : 512 * q + width] = part

    arrange(0)
    load.wait()
    for d in (1, 3, 2):
        wait(slots.at[pl.ds(((x - d) % NX) * NY, NY)], slot_x_recv.at[d])
        arrange(d)

    def product(half):
        block = momentum[pl.ds(half * (ROWS // 2), ROWS // 2), :]
        return lax.dot_general(block, full_basis[...], ACROSS, preferred_element_type=F32)

    partial[other] = product(other)
    for e in FAR_FIRST + (0,):
        rows = pl.ds(((z + e) % NZ) * 16, 16)
        send(partial.at[other, rows], pair_in.at[rows], pair_send, pair_recv.at[e], sibling)
    later(pair_in, pair_send)
    partial[c] = product(c)
    for e in FAR_FIRST:
        rows = pl.ds(((z + e) % NZ) * 16, 16)
        wait(pair_in.at[rows], pair_recv.at[e])
        partial[c, rows, :] = partial[c, rows, :] + pair_in[rows, :]
        send(partial.at[c, rows], sum_in.at[e - 1], sum_send, sum_recv, at_z(e))
    later(sum_in, sum_send)
    rows = pl.ds(z * 16, 16)
    wait(pair_in.at[rows], pair_recv.at[0])
    total = partial[c, rows, :] + pair_in[rows, :]
    momentum_t[...] = momentum[...].T
    wait(sum_in, sum_recv)
    for d in range(NZ - 1):
        total = total + sum_in[d]
    projected[c, z] = total
    for d in FAR_FIRST:
        send(projected.at[c, z], projected.at[c, z], own_send, own_recv.at[d], at_z(d))
    later(sum_in, own_send)
    send(projected.at[c, z], projected.at[c, z], half_send, half_recv, sibling)
    for d in NEAR_FIRST:
        source = (z - d) % NZ
        wait(projected.at[c, source], own_recv.at[d])
        send(projected.at[c, source], projected.at[c, source], half_send, half_recv, sibling)

    def gram_of(half):
        rows = projected[half].reshape(ROWS // 2, RANK)
        return lax.dot_general(rows, rows, (((0,), (0,)), ((), ())), precision=HIGH, preferred_element_type=F32)

    gram = gram_of(c)
    wait(projected.at[other], half_recv)
    later(projected.at[c], half_send)

    proj = projected[...].reshape(ROWS, RANK)
    gram_buf[...] = (gram + gram_of(other)).reshape(8, 16, RANK)
    for d in range(1, NX):
        send(gram_buf.at[2 * ((x + d) % NX) + c], gram_x.at[d - 1], gx_send, gx_recv, at_x(d))
    later(gram_x, gx_send)

    hi = proj.astype(BF16)
    left = proj - hi.astype(F32)
    mid = left.astype(BF16)
    low = (left - mid.astype(F32)).astype(BF16)
    terms = jnp.concatenate([hi, mid, low], axis=1)
    for piece in range(NX):
        out = jnp.dot(
            momentum_t[QUARTER * piece : QUARTER * (piece + 1), :], terms, preferred_element_type=F32
        )
        out = out[:, :RANK] + out[:, RANK : 2 * RANK] + out[:, 2 * RANK :]
        for n in range(NSLOT):
            zq[piece, n, : min(SLOT, QUARTER - n * SLOT), :] = out[n * SLOT : (n + 1) * SLOT, :]
        zq[piece, NSLOT - 1, QUARTER - (NSLOT - 1) * SLOT :, :] = jnp.zeros((NSLOT * SLOT - QUARTER, RANK), F32)

    def send_slot(e):
        slot = (y + e) % NY
        step = 1 + 2 * (slot % 2)

        @pl.when(slot < NSLOT)
        def _():
            send(zq.at[(x + 2) % NX, slot], zfar.at[e], zx_send.at[0], zfar_recv.at[e], at_x(step))
            send(zq.at[(x + NX - step) % NX, slot], zx.at[0, slot], zx_send.at[1], zx_recv.at[e], at_x(NX - step))

    def pass_slot(e):
        slot = (y + e) % NY
        step = 1 + 2 * (slot % 2)
        target = (x + step) % NX

        @pl.when(slot < NSLOT)
        def _():
            wait(zfar.at[e], zfar_recv.at[e])
            zq[target, slot] = zq[target, slot] + zfar[e]
            send(zq.at[target, slot], zx.at[1, slot], zx_send.at[2], zx_recv.at[e], at_x(step))

    def reduce_slot(e):
        slot = (y + e) % NY

        @pl.when(slot < NSLOT)
        def _():
            wait(zx.at[pl.ds(0, 2), 0], zx_recv.at[e])
            zmid[slot] = zq[x, slot] + zx[0, slot] + zx[1, slot]
            if e:
                send(zmid.at[slot], zy.at[e - 1], zy_send.at[e], zy_recv, at_y(e))

        if e:
            later(zmid.at[0], zy_send.at[e], slot < NSLOT)

    slot_order = FAR_FIRST + (0,)
    for e in slot_order:
        send_slot(e)
    later(zfar.at[pl.ds(0, NSLOT)], zx_send.at[0])
    later(zx.at[0], zx_send.at[1])
    later(zx.at[1], zx_send.at[2])

    wait(gram_x, gx_recv)
    own = 2 * x + c
    gram_mid[...] = gram_buf[own] + gram_x[0] + gram_x[1] + gram_x[2]
    for d in FAR_FIRST:
        send(gram_mid, gram_y.at[d - 1], gy_send, gy_recv, at_y(d))
    later(gram_y, gy_send)
    for e in slot_order:
        pass_slot(e)
    for e in slot_order[:2]:
        reduce_slot(e)
    wait(gram_y, gy_recv)
    total = gram_mid[...]
    for d in range(NY - 1):
        total = total + gram_y[d]
    gram_full[own] = total
    for d in (2, 1, 3, 0):
        for core in (other, c):
            if d == 0 and core is c:
                continue
            device = (((x + d) % NX) * NY + y, z * 2 + core)
            send(gram_full.at[own], gram_full.at[own], ga_send, ga_recv, device)
    later(gram_full.at[pl.ds(0, 7)], ga_send)
    for e in slot_order[2:7]:
        reduce_slot(e)
    wait(gram_full.at[pl.ds(0, 7)], ga_recv)

    inverse = inverse_factor(gram_full[...].reshape(RANK, RANK))
    reduce_slot(0)
    holder = y < NSLOT

    @pl.when(holder)
    def _():
        wait(zy, zy_recv)
        total = zmid[y]
        for d in range(NY - 1):
            total = total + zy[d]
        mine = lax.dot_general(total, inverse, (((1,), (1,)), ((), ())), precision=HIGH, preferred_element_type=F32)
        mine = mine.astype(BF16)
        back[x, y] = mine
        for d in (2, 1, 3):
            send(back.at[x, y], back.at[x, y], t_send.at[0], tx_recv.at[d], at_x(d))
        for d in NEAR_FIRST:
            send(back.at[x, y], back.at[x, y], t_send.at[0], ty_recv.at[d], at_y(d))
        mine = mine.astype(F32)
        sq_t[...] = jnp.sum(mine * mine, axis=0, keepdims=True)

    @pl.when(jnp.logical_not(holder))
    def _():
        sq_t[...] = jnp.zeros_like(sq_t)

    for d in range(1, 2 * NZ):
        send(sq_t, sq_t_in.at[d - 1], sq_send.at[0], sq_recv.at[0], (f, (t + d) % (2 * NZ)))
    later(sq_t_in, sq_send.at[0])
    ortho = lax.dot_general(proj, inverse, (((1,), (1,)), ((), ())), precision=HIGH, preferred_element_type=F32)

    def relay(e):
        source = (y - e) % NY

        @pl.when(source < NSLOT)
        def _():
            wait(back.at[x, source], ty_recv.at[e])
            for d in (2, 1, 3):
                send(back.at[x, source], back.at[x, source], t_send.at[1], tx_recv.at[d], at_x(d))

    for e in NEAR_FIRST[:5]:
        relay(e)
    wait(sq_t_in, sq_recv.at[0])
    sq_f[...] = sq_t[...] + jnp.sum(sq_t_in[...], axis=0)
    for dy in FAR_FIRST + (0,):
        for dx in (2, 1, 3, 0):
            if dx or dy:
                device = (((x + dx) % NX) * NY + (y + dy) % NY, t)
                send(sq_f, sq_f_in.at[dx * NY + dy - 1], sq_send.at[1], sq_recv.at[1], device)
    later(sq_f_in, sq_send.at[1])
    for e in NEAR_FIRST[5:]:
        relay(e)
    later(slots.at[pl.ds(0, 10)], t_send.at[0], holder)
    later(slots.at[pl.ds(0, 18)], t_send.at[1], holder)
    later(slots.at[pl.ds(0, 21)], t_send.at[1], jnp.logical_not(holder))
    def gathered(d):
        piece = (x - d) % NX
        if d:
            wait(back.at[piece], tx_recv.at[d])
        whole[pl.ds(pl.multiple_of(piece * QUARTER, 32), QUARTER), :] = back[piece].reshape(NSLOT * SLOT, RANK)[:QUARTER, :]

    for d in (0, 1, 3, 2):
        gathered(d)
    feedback = lax.dot_general(ortho.astype(BF16), whole[...], ACROSS, preferred_element_type=F32)
    momentum_out[...] = (momentum[...].astype(F32) - 0.05 * feedback).astype(BF16)
    weights_load.wait()
    wait(sq_f_in, sq_recv.at[1])
    squares = sq_f[...] + jnp.sum(sq_f_in[...], axis=0)
    scale = lax.rsqrt(squares / FW + 1e-06)
    row = lax.broadcasted_iota(jnp.int32, (16, RANK), 0)
    col = lax.broadcasted_iota(jnp.int32, (16, RANK), 1)
    pick = (col == row + 4 * f) & (row < 4)
    left = jnp.concatenate([ortho * scale, pick.astype(F32)], axis=0).astype(BF16)
    result = lax.dot_general(left, whole[...], ACROSS, preferred_element_type=F32)
    weights_out[...] = weights[...] - 0.02 * math.sqrt(DW / RANK) * result[:ROWS]
    basis_out[...] = result[ROWS : ROWS + 4] * jnp.sum(jnp.where(pick, scale, 0.0), axis=1, keepdims=True)[:4]
    flush()


def place_kernel(weights, momentum, basis, weights_out, momentum_out, basis_out, sems):
    copies = [
        pltpu.make_async_copy(source, target, sems.at[i])
        for i, (source, target) in enumerate(((weights, weights_out), (momentum, momentum_out), (basis, basis_out)))
    ]
    for copy in copies:
        copy.start()
    for copy in copies:
        copy.wait()


def shards(momentum, weights, basis):
    vmem = pl.BlockSpec(memory_space=pltpu.VMEM)
    hbm = pl.BlockSpec(memory_space=pltpu.HBM)
    dma = pltpu.SemaphoreType.DMA
    weights_out, momentum_out, basis_out = pl.pallas_call(
        exchange_kernel,
        out_shape=(
            jax.ShapeDtypeStruct((ROWS, COLS), F32),
            jax.ShapeDtypeStruct((ROWS, COLS), BF16),
            jax.ShapeDtypeStruct((4, COLS), F32),
        ),
        in_specs=[hbm, hbm, hbm],
        out_specs=(vmem, vmem, vmem),
        scratch_shapes=[
            pltpu.VMEM((ROWS, COLS), BF16),
            pltpu.VMEM((COLS, ROWS), BF16),
            pltpu.VMEM((ROWS, COLS), F32),
            pltpu.VMEM((4, COLS), F32),
            pltpu.VMEM((16, 512), F32),
            pltpu.VMEM((32, 16, 512), BF16),
            pltpu.VMEM((RANK, COLS), BF16),
            pltpu.VMEM((2, ROWS // 2, RANK), F32),
            pltpu.VMEM((ROWS // 2, RANK), F32),
            pltpu.VMEM((NZ - 1, 16, RANK), F32),
            pltpu.VMEM((2, NZ, 16, RANK), F32),
            pltpu.VMEM((8, 16, RANK), F32),
            pltpu.VMEM((NX - 1, 16, RANK), F32),
            pltpu.VMEM((16, RANK), F32),
            pltpu.VMEM((NY - 1, 16, RANK), F32),
            pltpu.VMEM((8, 16, RANK), F32),
            pltpu.VMEM((NX, NSLOT, SLOT, RANK), F32),
            pltpu.VMEM((NY, SLOT, RANK), F32),
            pltpu.VMEM((2, NSLOT, SLOT, RANK), F32),
            pltpu.VMEM((NSLOT, SLOT, RANK), F32),
            pltpu.VMEM((NY - 1, SLOT, RANK), F32),
            pltpu.VMEM((NX, NSLOT, SLOT, RANK), BF16),
            pltpu.VMEM((COLS, RANK), BF16),
            pltpu.VMEM((1, RANK), F32),
            pltpu.VMEM((1, RANK), F32),
            pltpu.VMEM((2 * NZ - 1, 1, RANK), F32),
            pltpu.VMEM((NX * NY - 1, 1, RANK), F32),
            dma(()), dma(()), dma(()), dma((NY,)), dma((NX,)), dma(()), dma((NZ,)), dma(()), dma(()), dma(()),
            dma((NZ,)), dma(()), dma(()), dma(()), dma(()), dma(()), dma(()), dma(()), dma(()), dma(()),
            dma((NY,)), dma((NY,)), dma((3,)), dma(()), dma((NY,)), dma((NY,)), dma((NX,)), dma((2,)), dma((2,)), dma((2,)),
        ],
        compiler_params=pltpu.CompilerParams(
            collective_id=0, has_side_effects=True, vmem_limit_bytes=48 * 2**20
        ),
        name="exchange",
    )(*[pltpu.with_memory_space_constraint(a, pltpu.HBM) for a in (momentum, weights, basis.T)])
    weights_out, momentum_out, basis_out = pl.pallas_call(
        place_kernel,
        out_shape=(
            jax.ShapeDtypeStruct((ROWS, COLS), F32),
            jax.ShapeDtypeStruct((ROWS, COLS), BF16),
            jax.ShapeDtypeStruct((4, COLS), F32),
        ),
        in_specs=[pl.BlockSpec(memory_space=pl.ANY)] * 3,
        out_specs=(hbm, hbm, hbm),
        scratch_shapes=[dma((3,))],
        compiler_params=pltpu.CompilerParams(vmem_limit_bytes=2 * 2**20),
        name="place",
    )(weights_out, momentum_out, basis_out)
    return weights_out, momentum_out, basis_out.T


def solution(mesh):
    in_specs = (P("fsdp", "tensor"), P("fsdp", "tensor"), P("tensor", "fsdp"))
    out_specs = (P("fsdp", "tensor"), P("fsdp", "tensor"), P("tensor", "fsdp"))
    return jax.shard_map(shards, mesh=mesh, in_specs=in_specs, out_specs=out_specs, check_vma=False)
```

```python
import functools
import math

import jax
import jax.numpy as jnp
from jax import lax
from jax.experimental import pallas as pl
from jax.experimental.pallas import tpu as pltpu
from jax.sharding import PartitionSpec as P

DW = 8192
FW = 26624
RANK = 128
ROWS = 256
COLS = 1664
NX, NY, NZ = 4, 8, 8
QUARTER = COLS // NX
SLOT = 64
AHEAD = 3
NSLOT = 7
LAST = QUARTER - (NSLOT - 1) * SLOT
FAR_FIRST = (4, 3, 5, 2, 6, 1, 7)
NEAR_FIRST = (1, 7, 2, 6, 3, 5, 4)

HIGH = lax.Precision.HIGHEST
ACROSS = (((1,), (1,)), ((), ()))
MESH = pl.DeviceIdType.MESH
F32 = jnp.float32
BF16 = jnp.bfloat16


def spread_row(a, k):
    return jnp.broadcast_to(a[k : k + 1, :], a.shape)


def inverse_factor(gram):
    lane = lax.broadcasted_iota(jnp.int32, (8, RANK), 1)
    sub = lax.broadcasted_iota(jnp.int32, (8, RANK), 0)
    lanes = lax.broadcasted_iota(jnp.int32, (RANK, RANK), 1)
    panels = [gram[8 * i : 8 * i + 8] for i in range(AHEAD + 1)]
    rest = gram[8 * (AHEAD + 1) :]
    done = []
    for first in range(0, RANK, 8):
        last = first + 8
        inside = (lane >= first) & (lane < last)

        def columns(panel):
            return [jnp.broadcast_to(panel[:, first + k : first + k + 1], (8, RANK)) for k in range(8)]

        block = columns(panels[0])
        below = [columns(panel) for panel in panels[1:]]
        rows = jnp.where(inside, jnp.where(lane - first == sub, 1.0, 0.0), panels[0])
        panels = [jnp.where(inside, 0.0, panel) for panel in panels[1:]]
        pivots = None
        for k in range(8):
            pivot = spread_row(block[k], k)
            inv = 1.0 / pivot
            pivots = pivot if pivots is None else jnp.where(sub == k, pivot, pivots)
            row = spread_row(rows, k)
            mult = jnp.where(sub > k, block[k] * inv, 0.0)
            entries = {n: spread_row(block[n], k) for n in range(k + 1, 8)}
            for n in entries:
                block[n] = block[n] - mult * entries[n]
            rows = rows - mult * row
            for i, column in enumerate(below):
                mult = column[k] * inv
                for n in entries:
                    column[n] = column[n] - mult * entries[n]
                panels[i] = panels[i] - mult * row
        rows = rows * lax.rsqrt(pivots)
        done.append(jnp.where(lane < last, rows, 0.0))
        start = last + 8 * AHEAD
        if start < RANK:
            upper = jnp.where(lane >= start, rows, 0.0)
            base = jnp.where((lanes[start:] >= first) & (lanes[start:] < last), 0.0, rest)
            change = lax.dot_general(upper, rows, (((0,), (0,)), ((), ())), precision=HIGH, preferred_element_type=F32)
            rest = base - change[start:, :]
            panels.append(rest[:8])
            rest = rest[8:]
    return jnp.concatenate(done, axis=0)


def exchange_kernel(
    momentum_hbm, weights_hbm, basis_hbm, weights_out, momentum_out, basis_out,
    momentum, momentum_t, weights, basis, stage, slots, full_basis, partial, pair_in, sum_in, projected, gram_buf, gram_x, gram_mid, gram_y, gram_full,
    zq, zfar, zx, zmid, zy, back, whole, sq_t, sq_f, sq_t_in, sq_f_in,
    load_sem, weights_sem, basis_sem, slot_y_recv, slot_x_recv, slot_send, pair_recv, pair_send, sum_recv, sum_send,
    own_recv, own_send, half_recv, half_send, gx_recv, gx_send, gy_recv, gy_send, ga_recv, ga_send,
    zfar_recv, zx_recv, zx_send, zy_recv, zy_send, ty_recv, tx_recv, t_send, sq_recv, sq_send,
):
    f, t = lax.axis_index("fsdp"), lax.axis_index("tensor")
    x, y = f // NY, f % NY
    z, c = t // 2, t % 2
    other = 1 - c
    pending = []

    def at_y(d):
        return (x * NY + (y + d) % NY, t)

    def at_x(d):
        return (((x + d) % NX) * NY + y, t)

    def at_z(d):
        return (f, ((z + d) % NZ) * 2 + c)

    sibling = (f, z * 2 + other)

    def send(src, dst, send_sem, recv_sem, device):
        pltpu.make_async_remote_copy(
            src_ref=src, dst_ref=dst, send_sem=send_sem, recv_sem=recv_sem, device_id=device, device_id_type=MESH
        ).start()

    def wait(ref, sem):
        pltpu.make_async_copy(ref, ref, sem).wait()

    def later(ref, sem, needed=None):
        pending.append((ref, sem, needed))

    def flush():
        for ref, sem, needed in pending:
            if needed is None:
                wait(ref, sem)
            else:
                pl.when(needed)(functools.partial(wait, ref, sem))

    basis_load = pltpu.make_async_copy(basis_hbm, basis, basis_sem)
    basis_load.start()
    barrier = pltpu.get_barrier_semaphore()
    everyone = [at(d) for d in FAR_FIRST for at in (at_y, at_z)] + [at_x(d) for d in (2, 1, 3)] + [sibling]
    for device in everyone:
        pl.semaphore_signal(barrier, inc=1, device_id=device, device_id_type=MESH)
    load = pltpu.make_async_copy(momentum_hbm, momentum, load_sem)
    load.start()
    weights_load = pltpu.make_async_copy(weights_hbm, weights, weights_sem)
    weights_load.start()

    stage[...] = jnp.zeros_like(stage)
    basis_load.wait()
    for q in range(4):
        width = min(512, COLS - 512 * q)
        stage[4 * q : 4 * q + 4, :width] = basis[:, 512 * q : 512 * q + width]
    slots[f] = stage[...].astype(BF16)
    pl.semaphore_wait(barrier, len(everyone))

    for d in (2, 1, 3):
        send(slots.at[f], slots.at[f], slot_send, slot_x_recv.at[d], at_x(d))
    for d in NEAR_FIRST:
        send(slots.at[f], slots.at[f], slot_send, slot_y_recv.at[d], at_y(d))
    for e in NEAR_FIRST:
        source = x * NY + (y - e) % NY
        wait(slots.at[source], slot_y_recv.at[e])
        for d in (2, 1, 3):
            send(slots.at[source], slots.at[source], slot_send, slot_x_recv.at[d], at_x(d))
    later(slots.at[pl.ds(0, 31)], slot_send)
    to_row = lax.broadcasted_iota(jnp.int32, (NY * 4, RANK), 0)
    from_row = lax.broadcasted_iota(jnp.int32, (NY * 4, RANK), 1)

    def arrange(d):
        group = (x - d) % NX
        flat = slots[pl.ds(group * NY, NY)].reshape(RANK, 512)
        for q in range(4):
            width = min(512, COLS - 512 * q)
            pick = (from_row == (to_row // 4) * 16 + 4 * q + to_row % 4).astype(F32).astype(BF16)
            part = jnp.dot(pick, flat[:, :width], preferred_element_type=F32).astype(BF16)
            full_basis[pl.ds(pl.multiple_of(group * NY * 4, 32), NY * 4), 512 * q : 512 * q + width] = part

    arrange(0)
    load.wait()
    for d in (1, 3, 2):
        wait(slots.at[pl.ds(((x - d) % NX) * NY, NY)], slot_x_recv.at[d])
        arrange(d)

    def product(half):
        block = momentum[pl.ds(half * (ROWS // 2), ROWS // 2), :]
        return lax.dot_general(block, full_basis[...], ACROSS, preferred_element_type=F32)

    partial[other] = product(other)
    for e in FAR_FIRST + (0,):
        rows = pl.ds(((z + e) % NZ) * 16, 16)
        send(partial.at[other, rows], pair_in.at[rows], pair_send, pair_recv.at[e], sibling)
    later(pair_in, pair_send)
    partial[c] = product(c)
    for e in FAR_FIRST:
        rows = pl.ds(((z + e) % NZ) * 16, 16)
        wait(pair_in.at[rows], pair_recv.at[e])
        partial[c, rows, :] = partial[c, rows, :] + pair_in[rows, :]
        send(partial.at[c, rows], sum_in.at[e - 1], sum_send, sum_recv, at_z(e))
    later(sum_in, sum_send)
    rows = pl.ds(z * 16, 16)
    wait(pair_in.at[rows], pair_recv.at[0])
    total = partial[c, rows, :] + pair_in[rows, :]
    momentum_t[...] = momentum[...].T
    wait(sum_in, sum_recv)
    for d in range(NZ - 1):
        total = total + sum_in[d]
    projected[c, z] = total
    for d in FAR_FIRST:
        send(projected.at[c, z], projected.at[c, z], own_send, own_recv.at[d], at_z(d))
    later(sum_in, own_send)
    send(projected.at[c, z], projected.at[c, z], half_send, half_recv, sibling)
    for d in NEAR_FIRST:
        source = (z - d) % NZ
        wait(projected.at[c, source], own_recv.at[d])
        send(projected.at[c, source], projected.at[c, source], half_send, half_recv, sibling)
    wait(projected.at[other], half_recv)
    later(projected.at[c], half_send)

    proj = projected[...].reshape(ROWS, RANK)
    gram = lax.dot_general(proj, proj, (((0,), (0,)), ((), ())), precision=HIGH, preferred_element_type=F32)
    gram_buf[...] = gram.reshape(8, 16, RANK)
    for d in range(1, NX):
        send(gram_buf.at[2 * ((x + d) % NX) + c], gram_x.at[d - 1], gx_send, gx_recv, at_x(d))
    later(gram_x, gx_send)

    hi = proj.astype(BF16)
    left = proj - hi.astype(F32)
    mid = left.astype(BF16)
    low = (left - mid.astype(F32)).astype(BF16)
    terms = jnp.concatenate([hi, mid, low], axis=1)
    for piece in range(NX):
        out = jnp.dot(
            momentum_t[QUARTER * piece : QUARTER * (piece + 1), :], terms, preferred_element_type=F32
        )
        out = out[:, :RANK] + out[:, RANK : 2 * RANK] + out[:, 2 * RANK :]
        for n in range(NSLOT):
            zq[piece, n, : min(SLOT, QUARTER - n * SLOT), :] = out[n * SLOT : (n + 1) * SLOT, :]
        zq[piece, NSLOT - 1, QUARTER - (NSLOT - 1) * SLOT :, :] = jnp.zeros((NSLOT * SLOT - QUARTER, RANK), F32)

    def send_slot(e):
        slot = (y + e) % NY
        step = 1 + 2 * (slot % 2)

        @pl.when(slot < NSLOT)
        def _():
            send(zq.at[(x + 2) % NX, slot], zfar.at[e], zx_send.at[0], zfar_recv.at[e], at_x(step))
            send(zq.at[(x + NX - step) % NX, slot], zx.at[0, slot], zx_send.at[1], zx_recv.at[e], at_x(NX - step))

    def pass_slot(e):
        slot = (y + e) % NY
        step = 1 + 2 * (slot % 2)
        target = (x + step) % NX

        @pl.when(slot < NSLOT)
        def _():
            wait(zfar.at[e], zfar_recv.at[e])
            zq[target, slot] = zq[target, slot] + zfar[e]
            send(zq.at[target, slot], zx.at[1, slot], zx_send.at[2], zx_recv.at[e], at_x(step))

    def reduce_slot(e):
        slot = (y + e) % NY

        @pl.when(slot < NSLOT)
        def _():
            wait(zx.at[pl.ds(0, 2), 0], zx_recv.at[e])
            zmid[slot] = zq[x, slot] + zx[0, slot] + zx[1, slot]
            if e:
                send(zmid.at[slot], zy.at[e - 1], zy_send.at[e], zy_recv, at_y(e))

        if e:
            later(zmid.at[0], zy_send.at[e], slot < NSLOT)

    slot_order = FAR_FIRST + (0,)
    for e in slot_order:
        send_slot(e)
    later(zfar.at[pl.ds(0, NSLOT)], zx_send.at[0])
    later(zx.at[0], zx_send.at[1])
    later(zx.at[1], zx_send.at[2])

    wait(gram_x, gx_recv)
    own = 2 * x + c
    gram_mid[...] = gram_buf[own] + gram_x[0] + gram_x[1] + gram_x[2]
    for d in FAR_FIRST:
        send(gram_mid, gram_y.at[d - 1], gy_send, gy_recv, at_y(d))
    later(gram_y, gy_send)
    for e in slot_order:
        pass_slot(e)
    for e in slot_order[:2]:
        reduce_slot(e)
    wait(gram_y, gy_recv)
    total = gram_mid[...]
    for d in range(NY - 1):
        total = total + gram_y[d]
    gram_full[own] = total
    for d in (2, 1, 3, 0):
        for core in (other, c):
            if d == 0 and core is c:
                continue
            device = (((x + d) % NX) * NY + y, z * 2 + core)
            send(gram_full.at[own], gram_full.at[own], ga_send, ga_recv, device)
    later(gram_full.at[pl.ds(0, 7)], ga_send)
    for e in slot_order[2:7]:
        reduce_slot(e)
    wait(gram_full.at[pl.ds(0, 7)], ga_recv)

    inverse = inverse_factor(gram_full[...].reshape(RANK, RANK))
    reduce_slot(0)
    holder = y < NSLOT

    @pl.when(holder)
    def _():
        wait(zy, zy_recv)
        total = zmid[y]
        for d in range(NY - 1):
            total = total + zy[d]
        mine = lax.dot_general(total, inverse, (((1,), (1,)), ((), ())), precision=HIGH, preferred_element_type=F32)
        mine = mine.astype(BF16)
        back[x, y] = mine

        def spread(slot):
            for d in (2, 1, 3):
                send(slot, slot, t_send.at[0], tx_recv.at[d], at_x(d))
            for d in NEAR_FIRST:
                send(slot, slot, t_send.at[0], ty_recv.at[d], at_y(d))

        pl.when(y < NSLOT - 1)(lambda: spread(back.at[x, y]))
        pl.when(y == NSLOT - 1)(lambda: spread(back.at[x, NSLOT - 1, pl.ds(0, LAST)]))
        mine = mine.astype(F32)
        sq_t[...] = jnp.sum(mine * mine, axis=0, keepdims=True)

    @pl.when(jnp.logical_not(holder))
    def _():
        sq_t[...] = jnp.zeros_like(sq_t)

    for d in range(1, 2 * NZ):
        send(sq_t, sq_t_in.at[d - 1], sq_send.at[0], sq_recv.at[0], (f, (t + d) % (2 * NZ)))
    later(sq_t_in, sq_send.at[0])
    ortho = lax.dot_general(proj, inverse, (((1,), (1,)), ((), ())), precision=HIGH, preferred_element_type=F32)

    def relay(e):
        source = (y - e) % NY

        def step(slot):
            wait(slot, ty_recv.at[e])
            for d in (2, 1, 3):
                send(slot, slot, t_send.at[1], tx_recv.at[d], at_x(d))

        pl.when(source < NSLOT - 1)(lambda: step(back.at[x, source]))
        pl.when(source == NSLOT - 1)(lambda: step(back.at[x, NSLOT - 1, pl.ds(0, LAST)]))

    for e in NEAR_FIRST[:6]:
        relay(e)
    wait(sq_t_in, sq_recv.at[0])
    sq_f[...] = sq_t[...] + jnp.sum(sq_t_in[...], axis=0)
    for dy in FAR_FIRST + (0,):
        for dx in (2, 1, 3, 0):
            if dx or dy:
                device = (((x + dx) % NX) * NY + (y + dy) % NY, t)
                send(sq_f, sq_f_in.at[dx * NY + dy - 1], sq_send.at[1], sq_recv.at[1], device)
    later(sq_f_in, sq_send.at[1])
    relay(NEAR_FIRST[6])
    later(whole.at[pl.ds(0, 10 * SLOT)], t_send.at[0], y < NSLOT - 1)
    later(whole.at[pl.ds(0, 10 * LAST)], t_send.at[0], y == NSLOT - 1)
    later(whole.at[pl.ds(0, 3 * (QUARTER - SLOT))], t_send.at[1], y < NSLOT - 1)
    later(whole.at[pl.ds(0, 3 * (QUARTER - LAST))], t_send.at[1], y == NSLOT - 1)
    later(whole.at[pl.ds(0, 3 * QUARTER)], t_send.at[1], jnp.logical_not(holder))
    def gathered(d):
        piece = (x - d) % NX
        if d:
            wait(whole.at[pl.ds(0, QUARTER)], tx_recv.at[d])
        whole[pl.ds(pl.multiple_of(piece * QUARTER, 32), QUARTER), :] = back[piece].reshape(NSLOT * SLOT, RANK)[:QUARTER, :]

    for d in (0, 1, 3, 2):
        gathered(d)
    feedback = lax.dot_general(ortho.astype(BF16), whole[...], ACROSS, preferred_element_type=F32)
    momentum_out[...] = (momentum[...].astype(F32) - 0.05 * feedback).astype(BF16)
    weights_load.wait()
    wait(sq_f_in, sq_recv.at[1])
    squares = sq_f[...] + jnp.sum(sq_f_in[...], axis=0)
    scale = lax.rsqrt(squares / FW + 1e-06)
    row = lax.broadcasted_iota(jnp.int32, (16, RANK), 0)
    col = lax.broadcasted_iota(jnp.int32, (16, RANK), 1)
    pick = (col == row + 4 * f) & (row < 4)
    left = jnp.concatenate([ortho * scale, pick.astype(F32)], axis=0).astype(BF16)
    result = lax.dot_general(left, whole[...], ACROSS, preferred_element_type=F32)
    weights_out[...] = weights[...] - 0.02 * math.sqrt(DW / RANK) * result[:ROWS]
    basis_out[...] = result[ROWS : ROWS + 4] * jnp.sum(jnp.where(pick, scale, 0.0), axis=1, keepdims=True)[:4]
    flush()


def place_kernel(weights, momentum, basis, weights_out, momentum_out, basis_out, sems):
    copies = [
        pltpu.make_async_copy(source, target, sems.at[i])
        for i, (source, target) in enumerate(((weights, weights_out), (momentum, momentum_out), (basis, basis_out)))
    ]
    for copy in copies:
        copy.start()
    for copy in copies:
        copy.wait()


def shards(momentum, weights, basis):
    vmem = pl.BlockSpec(memory_space=pltpu.VMEM)
    hbm = pl.BlockSpec(memory_space=pltpu.HBM)
    dma = pltpu.SemaphoreType.DMA
    weights_out, momentum_out, basis_out = pl.pallas_call(
        exchange_kernel,
        out_shape=(
            jax.ShapeDtypeStruct((ROWS, COLS), F32),
            jax.ShapeDtypeStruct((ROWS, COLS), BF16),
            jax.ShapeDtypeStruct((4, COLS), F32),
        ),
        in_specs=[hbm, hbm, hbm],
        out_specs=(vmem, vmem, vmem),
        scratch_shapes=[
            pltpu.VMEM((ROWS, COLS), BF16),
            pltpu.VMEM((COLS, ROWS), BF16),
            pltpu.VMEM((ROWS, COLS), F32),
            pltpu.VMEM((4, COLS), F32),
            pltpu.VMEM((16, 512), F32),
            pltpu.VMEM((32, 16, 512), BF16),
            pltpu.VMEM((RANK, COLS), BF16),
            pltpu.VMEM((2, ROWS // 2, RANK), F32),
            pltpu.VMEM((ROWS // 2, RANK), F32),
            pltpu.VMEM((NZ - 1, 16, RANK), F32),
            pltpu.VMEM((2, NZ, 16, RANK), F32),
            pltpu.VMEM((8, 16, RANK), F32),
            pltpu.VMEM((NX - 1, 16, RANK), F32),
            pltpu.VMEM((16, RANK), F32),
            pltpu.VMEM((NY - 1, 16, RANK), F32),
            pltpu.VMEM((8, 16, RANK), F32),
            pltpu.VMEM((NX, NSLOT, SLOT, RANK), F32),
            pltpu.VMEM((NY, SLOT, RANK), F32),
            pltpu.VMEM((2, NSLOT, SLOT, RANK), F32),
            pltpu.VMEM((NSLOT, SLOT, RANK), F32),
            pltpu.VMEM((NY - 1, SLOT, RANK), F32),
            pltpu.VMEM((NX, NSLOT, SLOT, RANK), BF16),
            pltpu.VMEM((COLS, RANK), BF16),
            pltpu.VMEM((1, RANK), F32),
            pltpu.VMEM((1, RANK), F32),
            pltpu.VMEM((2 * NZ - 1, 1, RANK), F32),
            pltpu.VMEM((NX * NY - 1, 1, RANK), F32),
            dma(()), dma(()), dma(()), dma((NY,)), dma((NX,)), dma(()), dma((NZ,)), dma(()), dma(()), dma(()),
            dma((NZ,)), dma(()), dma(()), dma(()), dma(()), dma(()), dma(()), dma(()), dma(()), dma(()),
            dma((NY,)), dma((NY,)), dma((3,)), dma(()), dma((NY,)), dma((NY,)), dma((NX,)), dma((2,)), dma((2,)), dma((2,)),
        ],
        compiler_params=pltpu.CompilerParams(
            collective_id=0, has_side_effects=True, vmem_limit_bytes=48 * 2**20
        ),
        name="exchange",
    )(*[pltpu.with_memory_space_constraint(a, pltpu.HBM) for a in (momentum, weights, basis.T)])
    weights_out, momentum_out, basis_out = pl.pallas_call(
        place_kernel,
        out_shape=(
            jax.ShapeDtypeStruct((ROWS, COLS), F32),
            jax.ShapeDtypeStruct((ROWS, COLS), BF16),
            jax.ShapeDtypeStruct((4, COLS), F32),
        ),
        in_specs=[pl.BlockSpec(memory_space=pl.ANY)] * 3,
        out_specs=(hbm, hbm, hbm),
        scratch_shapes=[dma((3,))],
        compiler_params=pltpu.CompilerParams(vmem_limit_bytes=2 * 2**20),
        name="place",
    )(weights_out, momentum_out, basis_out)
    return weights_out, momentum_out, basis_out.T


def solution(mesh):
    in_specs = (P("fsdp", "tensor"), P("fsdp", "tensor"), P("tensor", "fsdp"))
    out_specs = (P("fsdp", "tensor"), P("fsdp", "tensor"), P("tensor", "fsdp"))
    return jax.shard_map(shards, mesh=mesh, in_specs=in_specs, out_specs=out_specs, check_vma=False)
```
